256 devices in a mesh: node: 8 (over z_lo, x), sht: 32 (over y, z_hi, core).
Axes of the slice: x: 4, y: 4, z: 8 (z_hi: 4, z_lo: 2; z = z_hi * 2 + z_lo), core: 2. Of those that a mesh axis runs over, the one named last changes fastest.
Arguments:
- harmonics: bfloat16 [128, 32, 2, 2048], P('sht'), may hold values from -6 to 6
- radial: float32 [16, 2, 2048], P('node'), may hold values from -6 to 6
- node_weight: float32 [16], P('node'), may hold values from 0.3 to 3
- legendre: bfloat16 [128, 2048, 512], P('sht'), may hold values from -0.125 to 0.125
- order_table: int32 [128], replicated, may hold values from 0 to 2047, as said below
- cycle_table: int32 [512], P('sht'), may hold values from 1024 to 3072, as said below
Outputs:
- gradient: float32 [128, 32, 2, 2048], P('sht', 'node')
The draws below stay inside these ranges and needn't reach their ends.
Inputs may be any that keep to these rules, and one draw needn't show every extreme that they name: `order_table`: distinct orders; 0 and 2047 always among them. `cycle_table`: distinct cycle numbers of the equatorial belt; 1024 and 3072 always among them.
All inputs are finite; a program needn't handle non-finite values.
Results may differ from the reference program's by a relative error of at most 0.0059.
Values may be sent and summed in bfloat16 or wider, within the bound.
No kernel may reach another device: no remote copies, remote signals or barrier semaphores. Data moves between devices by JAX's collectives and lax.ppermute only.
A program may use at most 192 MiB of HBM per device.

```python
import math
import jax
import jax.numpy as jnp
from jax import lax

DEGREES = 2048
NSIDE = 1024
NPHI = 4096
ORDERS = 128
CYCLES = 512
NODES = 16
SIMS = 32


def distinct_with_ends(key, count, first, last):
    middle_values = jax.random.permutation(key, last - first - 1)[:count - 2] + first + 1
    chosen = jnp.concatenate([jnp.array([first, last], jnp.int32), middle_values.astype(jnp.int32)], 0)
    reorder = jax.random.permutation(jax.random.fold_in(key, 7), count)
    return chosen[reorder].astype(jnp.int32)


def draw_order_table(key, part):
    key = jax.random.fold_in(key, 11)
    return distinct_with_ends(key, ORDERS, 0, DEGREES - 1)


def draw_cycle_table(key, part):
    key = jax.random.fold_in(key, 23)
    return distinct_with_ends(key, CYCLES, NSIDE, 3 * NSIDE)


def block_levels(stream_key, extent, split, low, top_value):
    gain, own = 1.0, jax.random.fold_in(stream_key, 6)
    for axis_at, blocks in split:
        draws = jnp.exp(jax.random.uniform(jax.random.fold_in(own, axis_at), (blocks,), jnp.float32, low / len(split), top_value / len(split)))
        gain = gain * jnp.repeat(draws, extent[axis_at] // blocks).reshape([-1 if axis == axis_at else 1 for axis in range(len(extent))])
    return gain


def bell_draw(rng, shape, width, limit, cuts=(), held_as=jnp.bfloat16):
    drawn = width * jax.random.normal(rng, shape, jnp.float32)
    if cuts:
        drawn = drawn * block_levels(rng, shape, cuts, -0.22, 0.18)
    return jnp.clip(drawn, -limit, limit).astype(held_as)


def setup_inputs(seed: int = 0) -> dict:
    key_of = jax.random.split(jax.random.key(seed), 7)
    harmonics = bell_draw(key_of[0], (ORDERS, SIMS, 2, DEGREES), 1.0, 6.0, ((0, 32),))
    radial = bell_draw(key_of[1], (NODES, 2, DEGREES), 1.0, 6.0, ((0, 8),), jnp.float32)
    node_weight = jnp.clip(jnp.exp(math.log(3.0) - 2.3025851 * jax.random.uniform(key_of[2], (NODES,), jnp.float32) ** block_levels(key_of[2], (NODES,), ((0, 8),), -0.2, 0.2)), 0.3, 3.0)
    legendre = bell_draw(key_of[3], (ORDERS, DEGREES, CYCLES), DEGREES ** -0.5, 0.125, ((0, 32),))
    order_table = draw_order_table(jax.random.fold_in(key_of[6], 71), 0)
    cycle_table = draw_cycle_table(jax.random.fold_in(key_of[6], 71), 0)
    return {"harmonics": harmonics, "radial": radial, "node_weight": node_weight, "legendre": legendre, "order_table": order_table, "cycle_table": cycle_table}


def rounded(value):
    return lax.optimization_barrier(value.astype(jnp.bfloat16)).astype(jnp.float32)

def fourier_tables(order_table, pixels):
    pixel_index = jnp.arange(pixels, dtype=jnp.int32)
    product_index = order_table[:, None] * pixel_index[None, :] % pixels
    phase_angle = product_index.astype(jnp.float32) * (2.0 * math.pi / pixels)
    return (jnp.cos(phase_angle).astype(jnp.bfloat16), jnp.sin(phase_angle).astype(jnp.bfloat16))

def cycle_rotation(order_table, cycle_table, pixels):
    parity = (cycle_table - NSIDE + 1) % 2
    product_index = order_table[:, None] * (2 - parity)[None, :] % (2 * pixels)
    phase_angle = product_index.astype(jnp.float32) * (math.pi / pixels)
    return (jnp.cos(phase_angle), jnp.sin(phase_angle))

def reference(harmonics, radial, node_weight, legendre, order_table, cycle_table):
    cosines, sines = fourier_tables(order_table, NPHI)
    synth_table = jnp.concatenate([cosines, -sines], 0).astype(jnp.float32)
    analysis_table = jnp.concatenate([cosines, sines], 0).astype(jnp.float32)
    rot_cos, rot_sin = cycle_rotation(order_table, cycle_table, NPHI)
    rot_cos = rot_cos[:, :, None, None]
    rot_sin = rot_sin[:, :, None, None]
    legendre_f = legendre.astype(jnp.float32)
    harmonics_f = harmonics.astype(jnp.float32)

    def one_node(running, inputs):
        profile, weight = inputs
        weighted = rounded(harmonics_f[:, None] * profile[None, :, None, None, :])
        coefficients = rounded(jnp.einsum('olk,ofsrl->okfsr', legendre_f, weighted))
        real_part = rot_cos * coefficients[..., 0] - rot_sin * coefficients[..., 1]
        imag_part = rot_sin * coefficients[..., 0] + rot_cos * coefficients[..., 1]
        turned = rounded(jnp.concatenate([real_part, imag_part], 0))
        fields = jnp.einsum('hkfs,hj->kfsj', turned, synth_table) * ORDERS ** (-0.5)
        products = rounded(jnp.stack([fields[:, 1] * fields[:, 1], fields[:, 0] * fields[:, 1]], 1))
        spectra = jnp.einsum('kpsj,hj->hkps', products, analysis_table) * NPHI ** (-0.5)
        cos_part = spectra[:ORDERS]
        sin_part = spectra[ORDERS:]
        g_real = rot_cos * cos_part - rot_sin * sin_part
        g_imag = -(rot_sin * cos_part + rot_cos * sin_part)
        returned = rounded(jnp.stack([g_real, g_imag], -1))
        moments = jnp.einsum('olk,okpsr->olpsr', legendre_f, returned)
        node_term = weight * (profile[0][None, :, None, None] * moments[:, :, 0] + 2.0 * profile[1][None, :, None, None] * moments[:, :, 1])
        return (running + node_term, None)
    start_sum = jnp.zeros((ORDERS, DEGREES, SIMS, 2), jnp.float32)
    summed, _ = lax.scan(one_node, start_sum, (radial, node_weight))
    return jnp.transpose(summed * math.sqrt(DEGREES / CYCLES), (0, 2, 3, 1))
```

```python
import functools
import math

import jax
import jax.numpy as jnp
from jax import lax
from jax.experimental import pallas as pl
from jax.experimental.pallas import tpu as pltpu
from jax.sharding import PartitionSpec as P

NSIDE = 1024
F32 = jnp.float32
BF16 = jnp.bfloat16
LANES = 128


def announce_kernel(weight_ref, radial_ref, out_ref):
    rows = []
    for n in range(2):
        for p in range(2):
            rows.append(radial_ref[n, p : p + 1, :] * (weight_ref[n] * (2.0 * (p + 1))))
    rows = jnp.concatenate(rows, 0)
    for i in range(out_ref.shape[0]):
        out_ref[i] = rows


def announce(node_weight, radial, groups):
    return pl.pallas_call(
        announce_kernel,
        in_specs=[pl.BlockSpec(memory_space=pltpu.SMEM), pl.BlockSpec(memory_space=pltpu.VMEM)],
        out_shape=jax.ShapeDtypeStruct((groups, 4, radial.shape[2]), F32),
        name="announce",
    )(node_weight, radial)


def exchange_blocks(arrays):
    arrays = list(arrays)
    block = lax.broadcasted_iota(jnp.int32, arrays[0].shape, 1) // 16
    for bit in (1, 2, 4):
        low = block & bit == 0
        for i in range(8):
            if i & bit:
                continue
            a, b = arrays[i], arrays[i | bit]
            arrays[i] = jnp.where(low, a, pltpu.roll(b, 16 * bit, 1))
            arrays[i | bit] = jnp.where(low, pltpu.roll(a, LANES - 16 * bit, 1), b)
    return arrays


def forward_kernel(harm_ref, radial_ref, leg_ref, out_ref, lines, staged):
    order = pl.program_id(0)
    samples, degrees = harm_ref.shape[1], harm_ref.shape[3]
    nodes = radial_ref.shape[0]
    groups = samples // 4
    chunks = degrees // LANES
    held = harm_ref[0].astype(F32).reshape(samples * 2, degrees)
    for lane in range(chunks):
        lines[lane] = held[:, lane * LANES : (lane + 1) * LANES]
    weighted = []
    for part in range(2):
        own = jnp.concatenate(
            [
                jnp.concatenate(
                    [
                        lines[lane, pl.ds(s * 2 + part, groups, stride=8), :]
                        for lane in range(chunks)
                    ],
                    1,
                )
                for s in range(4)
            ],
            0,
        )
        for f in range(2):
            for n in range(nodes):
                weighted.append((own * radial_ref[n, f : f + 1, :]).astype(BF16))
    coefficients = jnp.dot(
        jnp.concatenate(weighted, 0), leg_ref[0], preferred_element_type=F32
    )
    rows = nodes * samples
    for o in range(4):

        @pl.when(order == o)
        def _():
            for part in range(2):
                for f in range(2):
                    at = (part * 2 + f) * rows
                    for lane in range(staged.shape[0]):
                        staged[lane, pl.ds(f * 8 + part * 4 + o, rows, stride=16), :] = (
                            coefficients[at : at + rows, lane * LANES : (lane + 1) * LANES]
                        )

    @pl.when(order == 3)
    def _():
        size = groups * 16
        for lane in range(staged.shape[0]):
            blocks = exchange_blocks([staged[lane, i * size : (i + 1) * size, :] for i in range(8)])
            for i in range(8):
                out_ref[lane * 8 + i] = blocks[i].astype(BF16).reshape(groups, 16, LANES)


def forward(harmonics, radial, legendre):
    orders_dev, samples, _, degrees = harmonics.shape
    nodes = radial.shape[0]
    cycles = legendre.shape[2]
    out = (cycles // LANES * nodes * 4, samples // 4, 16, LANES)
    return pl.pallas_call(
        forward_kernel,
        grid=(orders_dev,),
        in_specs=[
            pl.BlockSpec((1, samples, 2, degrees), lambda o: (o, 0, 0, 0)),
            pl.BlockSpec(radial.shape, lambda o: (0, 0, 0)),
            pl.BlockSpec((1, degrees, cycles), lambda o: (o, 0, 0)),
        ],
        out_specs=pl.BlockSpec(out, lambda o: (0, 0, 0, 0)),
        scratch_shapes=[
            pltpu.VMEM((degrees // LANES, samples * 2, LANES), F32),
            pltpu.VMEM((cycles // LANES, nodes * samples * 16, LANES), F32),
        ],
        out_shape=jax.ShapeDtypeStruct(out, BF16),
        compiler_params=pltpu.CompilerParams(vmem_limit_bytes=58 * 2**20),
        cost_estimate=pl.CostEstimate(
            flops=2 * orders_dev * 256 * degrees * cycles,
            bytes_accessed=legendre.size * 2 + 2**21,
            transcendentals=0,
        ),
        name="forward",
    )(harmonics, radial, legendre)


def table_kernel(ca_ref, sa_ref, cb_ref, sb_ref, cat_ref, sat_ref, cbt_ref, sbt_ref, out_ref, flip_ref):
    high = ca_ref.shape[0]
    low = cb_ref.shape[0]
    for a in range(high):
        out_ref[a * low : (a + 1) * low, :] = (
            ca_ref[a : a + 1, :] * cb_ref[...] - sa_ref[a : a + 1, :] * sb_ref[...]
        ).astype(BF16)
    wide = cbt_ref.shape[1]
    for a in range(cat_ref.shape[1]):
        flip_ref[:, a * wide : (a + 1) * wide] = (
            cat_ref[:, a : a + 1] * cbt_ref[...] - sat_ref[:, a : a + 1] * sbt_ref[...]
        ).astype(BF16)


def angle(index, period):
    phase = (index % period).astype(F32) * (2.0 * math.pi / period)
    return jnp.cos(phase), jnp.sin(phase)


def table_orders(order_table):
    grouped = order_table.reshape(-1, 1, 4)
    rows = jnp.broadcast_to(grouped, (grouped.shape[0], 2, 4)).reshape(-1)
    quarter = jnp.broadcast_to(
        jnp.arange(2, dtype=jnp.int32)[None, :, None], (grouped.shape[0], 2, 4)
    ).reshape(-1)
    return rows, quarter


def tables(order_table, pixels):
    rows, quarter = table_orders(order_table)
    low, wide = 64, 128
    shift = quarter * (pixels // 4)
    ca, sa = angle(jnp.arange(pixels // low, dtype=jnp.int32)[:, None] * low * rows[None], pixels)
    cb, sb = angle(jnp.arange(low, dtype=jnp.int32)[:, None] * rows[None] + shift[None], pixels)
    cat, sat = angle(rows[:, None] * (jnp.arange(pixels // wide, dtype=jnp.int32) * wide)[None], pixels)
    cbt, sbt = angle(
        rows[:, None] * jnp.arange(wide, dtype=jnp.int32)[None] + shift[:, None], pixels
    )
    count = rows.shape[0]
    return pl.pallas_call(
        table_kernel,
        out_shape=[
            jax.ShapeDtypeStruct((pixels, count), BF16),
            jax.ShapeDtypeStruct((count, pixels), BF16),
        ],
        compiler_params=pltpu.CompilerParams(vmem_limit_bytes=24 * 2**20),
        cost_estimate=pl.CostEstimate(
            flops=6 * pixels * count, bytes_accessed=4 * pixels * count, transcendentals=0
        ),
        name="tables",
    )(ca, sa, cb, sb, cat, sat, cbt, sbt)


def rotation(order_table, pixels):
    rows, quarter = table_orders(order_table)
    sign = (2 * quarter - 1).astype(F32)
    columns = []
    for parity in range(2):
        cosine, sine = angle(rows * (2 - parity), 2 * pixels)
        columns += [cosine, sign * sine]
    return jnp.stack(columns, 1)


def cell_kernel(in_ref, synth_ref, analysis_ref, turn_ref, parity_ref, out_ref, products, table, sem, *, block):
    count, pixels = analysis_ref.shape
    fetch = pltpu.make_async_copy(analysis_ref, table, sem)
    fetch.start()
    groups = in_ref.shape[1]
    step = products.shape[1] // (2 * LANES)
    width = step * LANES
    odd = jnp.broadcast_to(parity_ref[...], (count, LANES)) > 0.5
    turn = [jnp.broadcast_to(turn_ref[:, i : i + 1], (count, LANES)) for i in range(4)]
    rot_cos = jnp.where(odd, turn[2], turn[0])
    rot_sin = jnp.where(odd, turn[3], turn[1])
    scale = 1.0 / (128.0 * 64.0)
    back_cos = rot_cos * scale
    back_sin = rot_sin * scale

    def swap(x):
        grouped = x.reshape(count // 8, 8, LANES)
        return jnp.concatenate([grouped[:, 4:], grouped[:, :4]], 1).reshape(count, LANES)

    for first in range(0, groups, step):
        turned = [[], []]
        for g in range(first, first + step):
            arrived = in_ref[:, g].astype(F32)
            for f in range(2):
                x = arrived[:, f * 8 : (f + 1) * 8, :].reshape(count, LANES)
                turned[f].append((rot_cos * x + rot_sin * swap(x)).astype(BF16))
        turned = jnp.concatenate(turned[0] + turned[1], 1)
        for j in range(0, pixels, block):
            fields = jnp.dot(synth_ref[j : j + block, :], turned, preferred_element_type=F32)
            alpha, beta = fields[:, :width], fields[:, width:]
            products[j : j + block, :width] = (beta * beta).astype(BF16)
            products[j : j + block, width:] = (alpha * beta).astype(BF16)
        if first == 0:
            fetch.wait()
        spectra = jnp.dot(table[...], products[...], preferred_element_type=F32)
        for g in range(step):
            parts = []
            for p in range(2):
                at = p * width + g * LANES
                x = spectra[:, at : at + LANES]
                parts.append((back_cos * x - back_sin * swap(x)).reshape(count // 8, 8, LANES))
            out_ref[first + g] = jnp.concatenate(parts, 1).astype(BF16)


def cells(arrived, synth, analysis, turn, parity, step=4, block=512):
    owners, groups, rows, lanes = arrived.shape
    pixels, count = synth.shape
    whole = pl.BlockSpec(memory_space=pltpu.VMEM)
    return pl.pallas_call(
        functools.partial(cell_kernel, block=block),
        in_specs=[whole, whole, pl.BlockSpec(memory_space=pl.ANY), whole, whole],
        out_specs=whole,
        out_shape=jax.ShapeDtypeStruct((groups, owners, rows, lanes), BF16),
        scratch_shapes=[
            pltpu.VMEM((pixels, 2 * step * lanes), BF16),
            pltpu.VMEM((count, pixels), BF16),
            pltpu.SemaphoreType.DMA,
        ],
        compiler_params=pltpu.CompilerParams(vmem_limit_bytes=36 * 2**20),
        cost_estimate=pl.CostEstimate(
            flops=2 * 2 * pixels * count * groups * 2 * lanes,
            bytes_accessed=4 * pixels * count + 2**22,
            transcendentals=0,
        ),
        name="cells",
    )(arrived, synth, analysis, turn, parity)


def backward_kernel(in_ref, known_ref, leg_ref, out_ref, staged, profile):
    order = pl.program_id(0)
    degrees = leg_ref.shape[1]
    sources, cells_in = in_ref.shape[:2]
    chunks = staged.shape[0]
    per = cells_in // chunks
    rows = sources * per

    @pl.when(order == 0)
    def _():
        for lane in range(chunks):
            blocks = exchange_blocks(
                [
                    in_ref[:, lane * per + i].astype(F32).reshape(sources * 16, LANES)
                    for i in range(per)
                ]
            )
            for i in range(per):
                for group in range(sources):
                    staged[lane, pl.ds((group * per + i) * 16, 16), :] = blocks[i][
                        group * 16 : (group + 1) * 16
                    ]
        first = lax.broadcasted_iota(jnp.int32, (8, degrees), 0) < 4
        for group in range(sources):
            for p in range(2):
                lines = [
                    jnp.broadcast_to(known_ref[group, n * 2 + p : n * 2 + p + 1, :], (8, degrees))
                    for n in range(2)
                ]
                profile[p, group] = jnp.where(first, lines[0], lines[1])

    def picked(o):
        return jnp.concatenate(
            [
                jnp.concatenate(
                    [
                        staged[lane, pl.ds(p * 8 + part * 4 + o, rows, stride=16), :].astype(BF16)
                        for lane in range(chunks)
                    ],
                    1,
                )
                for part in range(2)
                for p in range(2)
            ],
            0,
        )

    taken = lax.switch(order, [functools.partial(picked, o) for o in range(4)])
    moments = lax.dot_general(
        taken, leg_ref[0], (((1,), (1,)), ((), ())), preferred_element_type=F32
    )
    moments = moments.reshape(2, 2, sources, 8, degrees)
    for part in range(2):
        total = jnp.sum(moments[part] * profile[...], (0, 1))
        out_ref[0, :, part, :] = total[:4] + total[4:]


def backward(at_orders, known, legendre):
    sources = at_orders.shape[0]
    orders_dev, degrees, cycles = legendre.shape
    return pl.pallas_call(
        backward_kernel,
        grid=(orders_dev,),
        in_specs=[
            pl.BlockSpec(at_orders.shape, lambda o: (0, 0, 0, 0)),
            pl.BlockSpec((sources, 4, degrees), lambda o: (0, 0, 0)),
            pl.BlockSpec((1, degrees, cycles), lambda o: (o, 0, 0)),
        ],
        out_specs=pl.BlockSpec((1, 4, 2, degrees), lambda o: (o, 0, 0, 0)),
        scratch_shapes=[
            pltpu.VMEM((cycles // LANES, sources * 8 * 16, LANES), F32),
            pltpu.VMEM((2, sources, 8, degrees), F32),
        ],
        out_shape=jax.ShapeDtypeStruct((orders_dev, 4, 2, degrees), F32),
        compiler_params=pltpu.CompilerParams(vmem_limit_bytes=44 * 2**20),
        cost_estimate=pl.CostEstimate(
            flops=2 * orders_dev * 256 * degrees * cycles,
            bytes_accessed=legendre.size * 2 + 2**21,
            transcendentals=0,
        ),
        name="backward",
    )(at_orders, known, legendre)


def on_device(harmonics, radial, node_weight, legendre, order_table, cycle_table):
    pixels = 4 * NSIDE
    groups = lax.axis_size("node")
    owners = lax.axis_size("sht")
    mine = announce(node_weight, radial, groups)
    harmonics, mine = lax.optimization_barrier((harmonics, mine))
    known = lax.all_to_all(mine, "node", 0, 0, tiled=True)
    outgoing = forward(harmonics, radial, legendre)
    outgoing, known = lax.optimization_barrier((outgoing, known))
    arrived = lax.all_to_all(outgoing, "sht", 0, 0, tiled=True)
    parity = jnp.tile(((cycle_table - NSIDE + 1) % 2).astype(F32), 8)[None]
    turn = rotation(order_table, pixels)
    synth, analysis = tables(order_table, pixels)
    returning = cells(arrived, synth, analysis, turn, parity)
    returning = returning.reshape(groups * owners, 16, LANES)
    at_orders = lax.all_to_all(returning, ("node", "sht"), 0, 0, tiled=True)
    at_orders = at_orders.reshape(groups, owners, 16, LANES)
    return backward(at_orders, known, legendre)


def solution(mesh):
    in_specs = (
        P("sht", None, None, None),
        P("node", None, None),
        P("node"),
        P("sht", None, None),
        P(),
        P("sht"),
    )
    out_specs = P("sht", "node", None, None)
    return jax.shard_map(
        on_device, mesh=mesh, in_specs=in_specs, out_specs=out_specs, check_vma=False
    )
```

```python
import functools
import math

import jax
import jax.numpy as jnp
from jax import lax
from jax.experimental import pallas as pl
from jax.experimental.pallas import tpu as pltpu
from jax.sharding import PartitionSpec as P

NSIDE = 1024
F32 = jnp.float32
BF16 = jnp.bfloat16
LANES = 128


def exchange_blocks(arrays):
    arrays = list(arrays)
    block = lax.broadcasted_iota(jnp.int32, arrays[0].shape, 1) // 16
    for bit in (1, 2, 4):
        low = block & bit == 0
        for i in range(8):
            if i & bit:
                continue
            a, b = arrays[i], arrays[i | bit]
            arrays[i] = jnp.where(low, a, pltpu.roll(b, 16 * bit, 1))
            arrays[i | bit] = jnp.where(low, pltpu.roll(a, LANES - 16 * bit, 1), b)
    return arrays


def forward_kernel(harm_ref, radial_ref, leg_ref, out_ref, lines, staged):
    order = pl.program_id(0)
    samples, degrees = harm_ref.shape[1], harm_ref.shape[3]
    nodes = radial_ref.shape[0]
    groups = samples // 4
    chunks = degrees // LANES
    held = harm_ref[0].astype(F32).reshape(samples * 2, degrees)
    for lane in range(chunks):
        lines[lane] = held[:, lane * LANES : (lane + 1) * LANES]
    weighted = []
    for part in range(2):
        own = jnp.concatenate(
            [
                jnp.concatenate(
                    [
                        lines[lane, pl.ds(s * 2 + part, groups, stride=8), :]
                        for lane in range(chunks)
                    ],
                    1,
                )
                for s in range(4)
            ],
            0,
        )
        for f in range(2):
            for n in range(nodes):
                weighted.append((own * radial_ref[n, f : f + 1, :]).astype(BF16))
    coefficients = jnp.dot(
        jnp.concatenate(weighted, 0), leg_ref[0], preferred_element_type=F32
    )
    rows = nodes * samples
    for o in range(4):

        @pl.when(order == o)
        def _():
            for part in range(2):
                for f in range(2):
                    at = (part * 2 + f) * rows
                    for lane in range(staged.shape[0]):
                        staged[lane, pl.ds(f * 8 + part * 4 + o, rows, stride=16), :] = (
                            coefficients[at : at + rows, lane * LANES : (lane + 1) * LANES]
                        )

    @pl.when(order == 3)
    def _():
        size = groups * 16
        for lane in range(staged.shape[0]):
            blocks = exchange_blocks([staged[lane, i * size : (i + 1) * size, :] for i in range(8)])
            for i in range(8):
                out_ref[lane * 8 + i] = blocks[i].astype(BF16).reshape(groups, 16, LANES)


def forward(harmonics, radial, legendre):
    orders_dev, samples, _, degrees = harmonics.shape
    nodes = radial.shape[0]
    cycles = legendre.shape[2]
    out = (cycles // LANES * nodes * 4, samples // 4, 16, LANES)
    return pl.pallas_call(
        forward_kernel,
        grid=(orders_dev,),
        in_specs=[
            pl.BlockSpec((1, samples, 2, degrees), lambda o: (o, 0, 0, 0)),
            pl.BlockSpec(radial.shape, lambda o: (0, 0, 0)),
            pl.BlockSpec((1, degrees, cycles), lambda o: (o, 0, 0)),
        ],
        out_specs=pl.BlockSpec(out, lambda o: (0, 0, 0, 0)),
        scratch_shapes=[
            pltpu.VMEM((degrees // LANES, samples * 2, LANES), F32),
            pltpu.VMEM((cycles // LANES, nodes * samples * 16, LANES), F32),
        ],
        out_shape=jax.ShapeDtypeStruct(out, BF16),
        compiler_params=pltpu.CompilerParams(vmem_limit_bytes=58 * 2**20),
        cost_estimate=pl.CostEstimate(
            flops=2 * orders_dev * 256 * degrees * cycles,
            bytes_accessed=legendre.size * 2 + 2**21,
            transcendentals=0,
        ),
        name="forward",
    )(harmonics, radial, legendre)


def table_kernel(ca_ref, sa_ref, cb_ref, sb_ref, cat_ref, sat_ref, cbt_ref, sbt_ref, out_ref, flip_ref):
    high = ca_ref.shape[0]
    low = cb_ref.shape[0]
    for a in range(high):
        out_ref[a * low : (a + 1) * low, :] = (
            ca_ref[a : a + 1, :] * cb_ref[...] - sa_ref[a : a + 1, :] * sb_ref[...]
        ).astype(BF16)
    wide = cbt_ref.shape[1]
    for a in range(cat_ref.shape[1]):
        flip_ref[:, a * wide : (a + 1) * wide] = (
            cat_ref[:, a : a + 1] * cbt_ref[...] - sat_ref[:, a : a + 1] * sbt_ref[...]
        ).astype(BF16)


def angle(index, period):
    phase = (index % period).astype(F32) * (2.0 * math.pi / period)
    return jnp.cos(phase), jnp.sin(phase)


def table_orders(order_table):
    grouped = order_table.reshape(-1, 1, 4)
    rows = jnp.broadcast_to(grouped, (grouped.shape[0], 2, 4)).reshape(-1)
    quarter = jnp.broadcast_to(
        jnp.arange(2, dtype=jnp.int32)[None, :, None], (grouped.shape[0], 2, 4)
    ).reshape(-1)
    return rows, quarter


def tables(order_table, pixels):
    rows, quarter = table_orders(order_table)
    low, wide = 64, 128
    shift = quarter * (pixels // 4)
    ca, sa = angle(jnp.arange(pixels // low, dtype=jnp.int32)[:, None] * low * rows[None], pixels)
    cb, sb = angle(jnp.arange(low, dtype=jnp.int32)[:, None] * rows[None] + shift[None], pixels)
    cat, sat = angle(rows[:, None] * (jnp.arange(pixels // wide, dtype=jnp.int32) * wide)[None], pixels)
    cbt, sbt = angle(
        rows[:, None] * jnp.arange(wide, dtype=jnp.int32)[None] + shift[:, None], pixels
    )
    count = rows.shape[0]
    return pl.pallas_call(
        table_kernel,
        out_shape=[
            jax.ShapeDtypeStruct((pixels, count), BF16),
            jax.ShapeDtypeStruct((count, pixels), BF16),
        ],
        compiler_params=pltpu.CompilerParams(vmem_limit_bytes=24 * 2**20),
        cost_estimate=pl.CostEstimate(
            flops=6 * pixels * count, bytes_accessed=4 * pixels * count, transcendentals=0
        ),
        name="tables",
    )(ca, sa, cb, sb, cat, sat, cbt, sbt)


def rotation(order_table, pixels):
    rows, quarter = table_orders(order_table)
    sign = (2 * quarter - 1).astype(F32)
    columns = []
    for parity in range(2):
        cosine, sine = angle(rows * (2 - parity), 2 * pixels)
        columns += [cosine, sign * sine]
    return jnp.stack(columns, 1)


def cell_kernel(in_ref, synth_ref, analysis_ref, turn_ref, parity_ref, out_ref, products, synth, analysis, sems, *, block):
    count, pixels = analysis_ref.shape
    fetch_synth = pltpu.make_async_copy(synth_ref, synth, sems.at[0])
    fetch_analysis = pltpu.make_async_copy(analysis_ref, analysis, sems.at[1])
    fetch_synth.start()
    fetch_analysis.start()
    groups = in_ref.shape[1]
    step = products.shape[1] // (2 * LANES)
    width = step * LANES
    odd = jnp.broadcast_to(parity_ref[...], (count, LANES)) > 0.5
    turn = [jnp.broadcast_to(turn_ref[:, i : i + 1], (count, LANES)) for i in range(4)]
    rot_cos = jnp.where(odd, turn[2], turn[0])
    rot_sin = jnp.where(odd, turn[3], turn[1])
    scale = 1.0 / (128.0 * 64.0)
    back_cos = rot_cos * scale
    back_sin = rot_sin * scale

    def swap(x):
        grouped = x.reshape(count // 8, 8, LANES)
        return jnp.concatenate([grouped[:, 4:], grouped[:, :4]], 1).reshape(count, LANES)

    for first in range(0, groups, step):
        turned = [[], []]
        for g in range(first, first + step):
            arrived = in_ref[:, g].astype(F32)
            for f in range(2):
                x = arrived[:, f * 8 : (f + 1) * 8, :].reshape(count, LANES)
                turned[f].append((rot_cos * x + rot_sin * swap(x)).astype(BF16))
        turned = jnp.concatenate(turned[0] + turned[1], 1)
        if first == 0:
            fetch_synth.wait()
        for j in range(0, pixels, block):
            fields = jnp.dot(synth[j : j + block, :], turned, preferred_element_type=F32)
            alpha, beta = fields[:, :width], fields[:, width:]
            products[j : j + block, :width] = (beta * beta).astype(BF16)
            products[j : j + block, width:] = (alpha * beta).astype(BF16)
        if first == 0:
            fetch_analysis.wait()
        spectra = jnp.dot(analysis[...], products[...], preferred_element_type=F32)
        for g in range(step):
            parts = []
            for p in range(2):
                at = p * width + g * LANES
                x = spectra[:, at : at + LANES]
                parts.append((back_cos * x - back_sin * swap(x)).reshape(count // 8, 8, LANES))
            out_ref[first + g] = jnp.concatenate(parts, 1).astype(BF16)


def cells(arrived, synth, analysis, turn, parity, step=4, block=512):
    owners, groups, rows, lanes = arrived.shape
    pixels, count = synth.shape
    whole = pl.BlockSpec(memory_space=pltpu.VMEM)
    anywhere = pl.BlockSpec(memory_space=pltpu.HBM)
    return pl.pallas_call(
        functools.partial(cell_kernel, block=block),
        in_specs=[whole, anywhere, anywhere, whole, whole],
        out_specs=whole,
        out_shape=jax.ShapeDtypeStruct((groups, owners, rows, lanes), BF16),
        scratch_shapes=[
            pltpu.VMEM((pixels, 2 * step * lanes), BF16),
            pltpu.VMEM((pixels, count), BF16),
            pltpu.VMEM((count, pixels), BF16),
            pltpu.SemaphoreType.DMA((2,)),
        ],
        compiler_params=pltpu.CompilerParams(vmem_limit_bytes=50 * 2**20),
        cost_estimate=pl.CostEstimate(
            flops=2 * 2 * pixels * count * groups * 2 * lanes,
            bytes_accessed=4 * pixels * count + 2**22,
            transcendentals=0,
        ),
        name="cells",
    )(arrived, synth, analysis, turn, parity)


def backward_kernel(
    place_ref, in_ref, near_ref, far_ref, leg_ref, out_ref, staged, profile, leg, sems
):
    step = pl.program_id(0)
    orders_dev, degrees = leg_ref.shape[:2]
    sources, cells_in = in_ref.shape[:2]
    chunks = staged.shape[0]
    per = cells_in // chunks
    rows = sources * per

    def fetch(o):
        return pltpu.make_async_copy(leg_ref.at[o], leg.at[o], sems.at[o])

    @pl.when(step == 0)
    def _():
        for o in range(orders_dev):
            fetch(o).start()

        def chunk(lane, carry):
            blocks = exchange_blocks(
                [
                    in_ref[:, lane * per + i].astype(F32).reshape(sources * 16, LANES)
                    for i in range(per)
                ]
            )
            for i in range(per):
                for group in range(sources):
                    staged[lane, pl.ds((group * per + i) * 16, 16), :] = blocks[i][
                        group * 16 : (group + 1) * 16
                    ]
            return carry

        lax.fori_loop(0, chunks, chunk, 0)
        first = lax.broadcasted_iota(jnp.int32, (8, degrees), 0) < 4
        for z, ref in enumerate((near_ref, far_ref)):
            for x in range(ref.shape[0]):
                group = (place_ref[0] ^ z) * 4 + (place_ref[1] ^ x)
                for p in range(2):
                    lines = [
                        jnp.broadcast_to(ref[x, n, p : p + 1, :], (8, degrees)) for n in range(2)
                    ]
                    profile[p, group] = jnp.where(first, lines[0], lines[1])

    @pl.when(step > 0)
    def _():
        o = step - 1
        taken = jnp.concatenate(
            [
                jnp.concatenate(
                    [
                        staged[lane, pl.ds(p * 8 + part * 4 + o, rows, stride=16), :].astype(BF16)
                        for lane in range(chunks)
                    ],
                    1,
                )
                for part in range(2)
                for p in range(2)
            ],
            0,
        )
        fetch(o).wait()
        moments = lax.dot_general(
            taken, leg[o], (((1,), (1,)), ((), ())), preferred_element_type=F32
        )
        moments = moments.reshape(2, 2, sources, 8, degrees)
        for part in range(2):
            total = jnp.sum(moments[part] * profile[...], (0, 1))
            out_ref[0, :, part, :] = total[:4] + total[4:]


def backward(place, at_orders, profiles, legendre):
    sources = at_orders.shape[0]
    orders_dev, degrees, cycles = legendre.shape
    near = profiles[0].shape
    return pl.pallas_call(
        backward_kernel,
        grid_spec=pltpu.PrefetchScalarGridSpec(
            num_scalar_prefetch=1,
            grid=(orders_dev + 1,),
            in_specs=[
                pl.BlockSpec(at_orders.shape, lambda o, place: (0, 0, 0, 0)),
                *[pl.BlockSpec(near, lambda o, place: (0, 0, 0, 0))] * 2,
                pl.BlockSpec(memory_space=pltpu.HBM),
            ],
            out_specs=pl.BlockSpec(
                (1, 4, 2, degrees), lambda o, place: (jnp.maximum(o - 1, 0), 0, 0, 0)
            ),
            scratch_shapes=[
                pltpu.VMEM((cycles // LANES, sources * 8 * 16, LANES), F32),
                pltpu.VMEM((2, sources, 8, degrees), F32),
                pltpu.VMEM(legendre.shape, BF16),
                pltpu.SemaphoreType.DMA((orders_dev,)),
            ],
        ),
        out_shape=jax.ShapeDtypeStruct((orders_dev, 4, 2, degrees), F32),
        compiler_params=pltpu.CompilerParams(vmem_limit_bytes=52 * 2**20),
        cost_estimate=pl.CostEstimate(
            flops=2 * orders_dev * 256 * degrees * cycles,
            bytes_accessed=legendre.size * 2 + 2**21,
            transcendentals=0,
        ),
        name="backward",
    )(place, at_orders, *profiles, legendre)


def swapped(value, bit):
    return lax.ppermute(value, "node", [(i, i ^ bit) for i in range(lax.axis_size("node"))])


def on_device(harmonics, radial, node_weight, legendre, order_table, cycle_table):
    pixels = 4 * NSIDE
    groups = lax.axis_size("node")
    owners = lax.axis_size("sht")
    outgoing = forward(harmonics, radial, legendre)
    outgoing, radial, node_weight, order_table, cycle_table = lax.optimization_barrier(
        (outgoing, radial, node_weight, order_table, cycle_table)
    )
    arrived = lax.all_to_all(outgoing, "sht", 0, 0, tiled=True)
    parity = jnp.tile(((cycle_table - NSIDE + 1) % 2).astype(F32), 8)[None]
    turn = rotation(order_table, pixels)
    synth, analysis = tables(order_table, pixels)
    radial, synth = lax.optimization_barrier((radial, synth))
    profile = radial * node_weight[:, None, None] * jnp.array([2.0, 4.0], F32)[None, :, None]
    near = jnp.stack([profile] + [swapped(profile, bit) for bit in (1, 2, 3)])
    arrived, near = lax.optimization_barrier((arrived, near))
    far = swapped(near, 4)
    returning = cells(arrived, synth, analysis, turn, parity)
    returning, far = lax.optimization_barrier((returning, far))
    returning = returning.reshape(groups * owners, 16, LANES)
    at_orders = lax.all_to_all(returning, ("node", "sht"), 0, 0, tiled=True)
    at_orders = at_orders.reshape(groups, owners, 16, LANES)
    node = lax.axis_index("node").astype(jnp.int32)
    place = jnp.stack([node // 4, node % 4])
    return backward(place, at_orders, (near, far), legendre)


def solution(mesh):
    in_specs = (
        P("sht", None, None, None),
        P("node", None, None),
        P("node"),
        P("sht", None, None),
        P(),
        P("sht"),
    )
    out_specs = P("sht", "node", None, None)
    return jax.shard_map(
        on_device, mesh=mesh, in_specs=in_specs, out_specs=out_specs, check_vma=False
    )
```

```python
import functools
import math

import jax
import jax.numpy as jnp
from jax import lax
from jax.experimental import pallas as pl
from jax.experimental.pallas import tpu as pltpu
from jax.sharding import PartitionSpec as P

NSIDE = 1024
F32 = jnp.float32
BF16 = jnp.bfloat16
LANES = 128


def exchange_blocks(arrays):
    arrays = list(arrays)
    block = lax.broadcasted_iota(jnp.int32, arrays[0].shape, 1) // 16
    for bit in (1, 2, 4):
        low = block & bit == 0
        for i in range(8):
            if i & bit:
                continue
            a, b = arrays[i], arrays[i | bit]
            arrays[i] = jnp.where(low, a, pltpu.roll(b, 16 * bit, 1))
            arrays[i | bit] = jnp.where(low, pltpu.roll(a, LANES - 16 * bit, 1), b)
    return arrays


def forward_kernel(harm_ref, radial_ref, leg_ref, out_ref, lines, staged):
    order = pl.program_id(0)
    samples, degrees = harm_ref.shape[1], harm_ref.shape[3]
    nodes = radial_ref.shape[0]
    groups = samples // 4
    chunks = degrees // LANES
    held = harm_ref[0].astype(F32).reshape(samples * 2, degrees)
    for lane in range(chunks):
        lines[lane] = held[:, lane * LANES : (lane + 1) * LANES]
    weighted = []
    for part in range(2):
        own = jnp.concatenate(
            [
                jnp.concatenate(
                    [
                        lines[lane, pl.ds(s * 2 + part, groups, stride=8), :]
                        for lane in range(chunks)
                    ],
                    1,
                )
                for s in range(4)
            ],
            0,
        )
        for f in range(2):
            for n in range(nodes):
                weighted.append((own * radial_ref[n, f : f + 1, :]).astype(BF16))
    coefficients = jnp.dot(
        jnp.concatenate(weighted, 0), leg_ref[0], preferred_element_type=F32
    )
    rows = nodes * samples
    for o in range(4):

        @pl.when(order == o)
        def _():
            for part in range(2):
                for f in range(2):
                    at = (part * 2 + f) * rows
                    for lane in range(staged.shape[0]):
                        staged[lane, pl.ds(f * 8 + part * 4 + o, rows, stride=16), :] = (
                            coefficients[at : at + rows, lane * LANES : (lane + 1) * LANES]
                        )

    @pl.when(order == 3)
    def _():
        size = groups * 16
        for lane in range(staged.shape[0]):
            blocks = exchange_blocks([staged[lane, i * size : (i + 1) * size, :] for i in range(8)])
            for i in range(8):
                out_ref[lane * 8 + i] = blocks[i].astype(BF16).reshape(groups, 16, LANES)


def forward(harmonics, radial, legendre):
    orders_dev, samples, _, degrees = harmonics.shape
    nodes = radial.shape[0]
    cycles = legendre.shape[2]
    out = (cycles // LANES * nodes * 4, samples // 4, 16, LANES)
    return pl.pallas_call(
        forward_kernel,
        grid=(orders_dev,),
        in_specs=[
            pl.BlockSpec((1, samples, 2, degrees), lambda o: (o, 0, 0, 0)),
            pl.BlockSpec(radial.shape, lambda o: (0, 0, 0)),
            pl.BlockSpec((1, degrees, cycles), lambda o: (o, 0, 0)),
        ],
        out_specs=pl.BlockSpec(out, lambda o: (0, 0, 0, 0)),
        scratch_shapes=[
            pltpu.VMEM((degrees // LANES, samples * 2, LANES), F32),
            pltpu.VMEM((cycles // LANES, nodes * samples * 16, LANES), F32),
        ],
        out_shape=jax.ShapeDtypeStruct(out, BF16),
        compiler_params=pltpu.CompilerParams(vmem_limit_bytes=58 * 2**20),
        cost_estimate=pl.CostEstimate(
            flops=2 * orders_dev * 256 * degrees * cycles,
            bytes_accessed=legendre.size * 2 + 2**21,
            transcendentals=0,
        ),
        name="forward",
    )(harmonics, radial, legendre)


def table_kernel(cat_ref, sat_ref, cbt_ref, sbt_ref, flip_ref):
    wide = cbt_ref.shape[1]
    for a in range(cat_ref.shape[1]):
        flip_ref[:, a * wide : (a + 1) * wide] = (
            cat_ref[:, a : a + 1] * cbt_ref[...] - sat_ref[:, a : a + 1] * sbt_ref[...]
        ).astype(BF16)


def angle(index, period):
    phase = (index % period).astype(F32) * (2.0 * math.pi / period)
    return jnp.cos(phase), jnp.sin(phase)


def table_orders(order_table):
    grouped = order_table.reshape(-1, 1, 4)
    rows = jnp.broadcast_to(grouped, (grouped.shape[0], 2, 4)).reshape(-1)
    quarter = jnp.broadcast_to(
        jnp.arange(2, dtype=jnp.int32)[None, :, None], (grouped.shape[0], 2, 4)
    ).reshape(-1)
    return rows, quarter


def tables(order_table, pixels):
    rows, quarter = table_orders(order_table)
    low, wide = 64, 128
    shift = quarter * (pixels // 4)
    ca, sa = angle(jnp.arange(pixels // low, dtype=jnp.int32)[:, None] * low * rows[None], pixels)
    cb, sb = angle(jnp.arange(low, dtype=jnp.int32)[:, None] * rows[None] + shift[None], pixels)
    cat, sat = angle(rows[:, None] * (jnp.arange(pixels // wide, dtype=jnp.int32) * wide)[None], pixels)
    cbt, sbt = angle(
        rows[:, None] * jnp.arange(wide, dtype=jnp.int32)[None] + shift[:, None], pixels
    )
    count = rows.shape[0]
    flipped = pl.pallas_call(
        table_kernel,
        out_shape=jax.ShapeDtypeStruct((count, pixels), BF16),
        compiler_params=pltpu.CompilerParams(vmem_limit_bytes=24 * 2**20),
        cost_estimate=pl.CostEstimate(
            flops=3 * pixels * count, bytes_accessed=2 * pixels * count, transcendentals=0
        ),
        name="tables",
    )(cat, sat, cbt, sbt)
    return (ca, sa), (cb, sb), flipped


def rotation(order_table, pixels):
    rows, quarter = table_orders(order_table)
    sign = (2 * quarter - 1).astype(F32)
    columns = []
    for parity in range(2):
        cosine, sine = angle(rows * (2 - parity), 2 * pixels)
        columns += [cosine, sign * sine]
    return jnp.stack(columns, 1)


def cell_kernel(
    in_ref, ca_ref, sa_ref, cb_ref, sb_ref, analysis_ref, turn_ref, parity_ref, out_ref, products, synth, analysis, sem, *, block
):
    count, pixels = analysis_ref.shape
    fetch_analysis = pltpu.make_async_copy(analysis_ref, analysis, sem)
    fetch_analysis.start()
    low = cb_ref.shape[0]
    groups = in_ref.shape[1]
    step = products.shape[1] // (2 * LANES)
    width = step * LANES
    odd = jnp.broadcast_to(parity_ref[...], (count, LANES)) > 0.5
    turn = [jnp.broadcast_to(turn_ref[:, i : i + 1], (count, LANES)) for i in range(4)]
    rot_cos = jnp.where(odd, turn[2], turn[0])
    rot_sin = jnp.where(odd, turn[3], turn[1])
    scale = 1.0 / (128.0 * 64.0)
    back_cos = rot_cos * scale
    back_sin = rot_sin * scale

    def swap(x):
        return pltpu.roll(x.reshape(count // 8, 8, LANES), 4, 1).reshape(count, LANES)

    for first in range(0, groups, step):
        turned = [[], []]
        for g in range(first, first + step):
            arrived = in_ref[:, g].astype(F32)
            for f in range(2):
                x = arrived[:, f * 8 : (f + 1) * 8, :].reshape(count, LANES)
                turned[f].append((rot_cos * x + rot_sin * swap(x)).astype(BF16))
        turned = jnp.concatenate(turned[0] + turned[1], 1)
        for j in range(0, pixels, block):
            if first == 0:
                for a in range(j // low, (j + block) // low):
                    synth[a * low : (a + 1) * low, :] = (
                        ca_ref[a : a + 1, :] * cb_ref[...] - sa_ref[a : a + 1, :] * sb_ref[...]
                    ).astype(BF16)
            fields = jnp.dot(synth[j : j + block, :], turned, preferred_element_type=F32)
            alpha, beta = fields[:, :width], fields[:, width:]
            products[j : j + block, :width] = (beta * beta).astype(BF16)
            products[j : j + block, width:] = (alpha * beta).astype(BF16)
        if first == 0:
            fetch_analysis.wait()
        spectra = jnp.dot(analysis[...], products[...], preferred_element_type=F32)
        for g in range(step):
            parts = []
            for p in range(2):
                at = p * width + g * LANES
                x = spectra[:, at : at + LANES]
                parts.append((back_cos * x - back_sin * swap(x)).reshape(count // 8, 8, LANES))
            out_ref[first + g] = jnp.concatenate(parts, 1).astype(BF16)


def cells(arrived, high, low, analysis, turn, parity, step=4, block=1024):
    owners, groups, rows, lanes = arrived.shape
    count, pixels = analysis.shape
    whole = pl.BlockSpec(memory_space=pltpu.VMEM)
    anywhere = pl.BlockSpec(memory_space=pltpu.HBM)
    return pl.pallas_call(
        functools.partial(cell_kernel, block=block),
        in_specs=[*[whole] * 5, anywhere, whole, whole],
        out_specs=whole,
        out_shape=jax.ShapeDtypeStruct((groups, owners, rows, lanes), BF16),
        scratch_shapes=[
            pltpu.VMEM((pixels, 2 * step * lanes), BF16),
            pltpu.VMEM((pixels, count), BF16),
            pltpu.VMEM((count, pixels), BF16),
            pltpu.SemaphoreType.DMA,
        ],
        compiler_params=pltpu.CompilerParams(vmem_limit_bytes=50 * 2**20),
        cost_estimate=pl.CostEstimate(
            flops=2 * 2 * pixels * count * groups * 2 * lanes,
            bytes_accessed=4 * pixels * count + 2**22,
            transcendentals=0,
        ),
        name="cells",
    )(arrived, *high, *low, analysis, turn, parity)


def backward_kernel(
    place_ref, in_ref, near_ref, far_ref, leg_ref, out_ref, staged, profile, leg, sems
):
    step = pl.program_id(0)
    orders_dev, degrees = leg_ref.shape[:2]
    sources, cells_in = in_ref.shape[:2]
    chunks = staged.shape[0]
    per = cells_in // chunks
    rows = sources * per

    def fetch(o):
        return pltpu.make_async_copy(leg_ref.at[o], leg.at[o], sems.at[o])

    @pl.when(step == 0)
    def _():
        for o in range(orders_dev):
            fetch(o).start()

        def chunk(lane, carry):
            blocks = exchange_blocks(
                [
                    in_ref[:, lane * per + i].astype(F32).reshape(sources * 16, LANES)
                    for i in range(per)
                ]
            )
            for i in range(per):
                for group in range(sources):
                    staged[lane, pl.ds((group * per + i) * 16, 16), :] = blocks[i][
                        group * 16 : (group + 1) * 16
                    ]
            return carry

        lax.fori_loop(0, chunks, chunk, 0)
        first = lax.broadcasted_iota(jnp.int32, (8, degrees), 0) < 4
        for z, ref in enumerate((near_ref, far_ref)):
            for x in range(ref.shape[0]):
                group = (place_ref[0] ^ z) * 4 + (place_ref[1] ^ x)
                for p in range(2):
                    lines = [
                        jnp.broadcast_to(ref[x, n, p : p + 1, :], (8, degrees)) for n in range(2)
                    ]
                    profile[p, group] = jnp.where(first, lines[0], lines[1])

    @pl.when(step > 0)
    def _():
        o = step - 1
        taken = jnp.concatenate(
            [
                jnp.concatenate(
                    [
                        staged[lane, pl.ds(p * 8 + part * 4 + o, rows, stride=16), :].astype(BF16)
                        for lane in range(chunks)
                    ],
                    1,
                )
                for part in range(2)
                for p in range(2)
            ],
            0,
        )
        fetch(o).wait()
        moments = lax.dot_general(
            taken, leg[o], (((1,), (1,)), ((), ())), preferred_element_type=F32
        )
        moments = moments.reshape(2, 2, sources, 8, degrees)
        for part in range(2):
            total = jnp.sum(moments[part] * profile[...], (0, 1))
            out_ref[0, :, part, :] = total[:4] + total[4:]


def backward(place, at_orders, profiles, legendre):
    sources = at_orders.shape[0]
    orders_dev, degrees, cycles = legendre.shape
    near = profiles[0].shape
    return pl.pallas_call(
        backward_kernel,
        grid_spec=pltpu.PrefetchScalarGridSpec(
            num_scalar_prefetch=1,
            grid=(orders_dev + 1,),
            in_specs=[
                pl.BlockSpec(at_orders.shape, lambda o, place: (0, 0, 0, 0)),
                *[pl.BlockSpec(near, lambda o, place: (0, 0, 0, 0))] * 2,
                pl.BlockSpec(memory_space=pltpu.HBM),
            ],
            out_specs=pl.BlockSpec(
                (1, 4, 2, degrees), lambda o, place: (jnp.maximum(o - 1, 0), 0, 0, 0)
            ),
            scratch_shapes=[
                pltpu.VMEM((cycles // LANES, sources * 8 * 16, LANES), F32),
                pltpu.VMEM((2, sources, 8, degrees), F32),
                pltpu.VMEM(legendre.shape, BF16),
                pltpu.SemaphoreType.DMA((orders_dev,)),
            ],
        ),
        out_shape=jax.ShapeDtypeStruct((orders_dev, 4, 2, degrees), F32),
        compiler_params=pltpu.CompilerParams(vmem_limit_bytes=52 * 2**20),
        cost_estimate=pl.CostEstimate(
            flops=2 * orders_dev * 256 * degrees * cycles,
            bytes_accessed=legendre.size * 2 + 2**21,
            transcendentals=0,
        ),
        name="backward",
    )(place, at_orders, *profiles, legendre)


def swapped(value, bit):
    return lax.ppermute(value, "node", [(i, i ^ bit) for i in range(lax.axis_size("node"))])


def on_device(harmonics, radial, node_weight, legendre, order_table, cycle_table):
    pixels = 4 * NSIDE
    groups = lax.axis_size("node")
    owners = lax.axis_size("sht")
    outgoing = forward(harmonics, radial, legendre)
    outgoing, radial, node_weight, order_table, cycle_table = lax.optimization_barrier(
        (outgoing, radial, node_weight, order_table, cycle_table)
    )
    arrived = lax.all_to_all(outgoing, "sht", 0, 0, tiled=True)
    parity = jnp.tile(((cycle_table - NSIDE + 1) % 2).astype(F32), 8)[None]
    turn = rotation(order_table, pixels)
    high, low, analysis = tables(order_table, pixels)
    radial, analysis = lax.optimization_barrier((radial, analysis))
    profile = radial * node_weight[:, None, None] * jnp.array([2.0, 4.0], F32)[None, :, None]
    near = jnp.stack([profile] + [swapped(profile, bit) for bit in (1, 2, 3)])
    arrived, near = lax.optimization_barrier((arrived, near))
    far = swapped(near, 4)
    returning = cells(arrived, high, low, analysis, turn, parity)
    returning, far = lax.optimization_barrier((returning, far))
    returning = returning.reshape(groups * owners, 16, LANES)
    at_orders = lax.all_to_all(returning, ("node", "sht"), 0, 0, tiled=True)
    at_orders = at_orders.reshape(groups, owners, 16, LANES)
    node = lax.axis_index("node").astype(jnp.int32)
    place = jnp.stack([node // 4, node % 4])
    return backward(place, at_orders, (near, far), legendre)


def solution(mesh):
    in_specs = (
        P("sht", None, None, None),
        P("node", None, None),
        P("node"),
        P("sht", None, None),
        P(),
        P("sht"),
    )
    out_specs = P("sht", "node", None, None)
    return jax.shard_map(
        on_device, mesh=mesh, in_specs=in_specs, out_specs=out_specs, check_vma=False
    )
```

```python
import functools
import math

import jax
import jax.numpy as jnp
from jax import lax
from jax.experimental import pallas as pl
from jax.experimental.pallas import tpu as pltpu
from jax.sharding import PartitionSpec as P

NSIDE = 1024
F32 = jnp.float32
BF16 = jnp.bfloat16
LANES = 128


def deal_blocks(arrays):
    arrays = [arrays[-i % 8] for i in range(8)]
    block = lax.broadcasted_iota(jnp.int32, arrays[0].shape, 1) // 16
    for bit in (1, 2, 4):
        moved = block & bit != 0
        arrays = [jnp.where(moved, arrays[(i - bit) % 8], arrays[i]) for i in range(8)]
    return arrays


def shift_blocks(value, count):
    return value if count == 0 else pltpu.roll(value, 16 * count, 1)


def forward_kernel(harm_ref, radial_ref, leg_ref, out_ref, lines, staged):
    order = pl.program_id(0)
    samples, degrees = harm_ref.shape[1], harm_ref.shape[3]
    nodes = radial_ref.shape[0]
    groups = samples // 4
    chunks = degrees // LANES
    held = harm_ref[0].astype(F32).reshape(samples * 2, degrees)
    for lane in range(chunks):
        lines[lane] = held[:, lane * LANES : (lane + 1) * LANES]
    weighted = []
    for part in range(2):
        own = jnp.concatenate(
            [
                jnp.concatenate(
                    [
                        lines[lane, pl.ds(s * 2 + part, groups, stride=8), :]
                        for lane in range(chunks)
                    ],
                    1,
                )
                for s in range(4)
            ],
            0,
        )
        for f in range(2):
            for n in range(nodes):
                weighted.append((own * radial_ref[n, f : f + 1, :]).astype(BF16))
    coefficients = jnp.dot(
        jnp.concatenate(weighted, 0), leg_ref[0], preferred_element_type=F32
    )
    rows = nodes * samples
    for o in range(4):

        @pl.when(order == o)
        def _():
            for part in range(2):
                for f in range(2):
                    at = (part * 2 + f) * rows
                    for lane in range(staged.shape[0]):
                        staged[lane, pl.ds(f * 8 + part * 4 + o, rows, stride=16), :] = (
                            coefficients[at : at + rows, lane * LANES : (lane + 1) * LANES]
                        )

    @pl.when(order == 3)
    def _():
        size = groups * 16
        for lane in range(staged.shape[0]):
            blocks = deal_blocks(
                [shift_blocks(staged[lane, i * size : (i + 1) * size, :], i) for i in range(8)]
            )
            for i in range(8):
                out_ref[lane * 8 + i] = blocks[i].astype(BF16).reshape(groups, 16, LANES)


def forward(harmonics, radial, legendre):
    orders_dev, samples, _, degrees = harmonics.shape
    nodes = radial.shape[0]
    cycles = legendre.shape[2]
    out = (cycles // LANES * nodes * 4, samples // 4, 16, LANES)
    return pl.pallas_call(
        forward_kernel,
        grid=(orders_dev,),
        in_specs=[
            pl.BlockSpec((1, samples, 2, degrees), lambda o: (o, 0, 0, 0)),
            pl.BlockSpec(radial.shape, lambda o: (0, 0, 0)),
            pl.BlockSpec((1, degrees, cycles), lambda o: (o, 0, 0)),
        ],
        out_specs=pl.BlockSpec(out, lambda o: (0, 0, 0, 0)),
        scratch_shapes=[
            pltpu.VMEM((degrees // LANES, samples * 2, LANES), F32),
            pltpu.VMEM((cycles // LANES, nodes * samples * 16, LANES), F32),
        ],
        out_shape=jax.ShapeDtypeStruct(out, BF16),
        compiler_params=pltpu.CompilerParams(vmem_limit_bytes=58 * 2**20),
        cost_estimate=pl.CostEstimate(
            flops=2 * orders_dev * 256 * degrees * cycles,
            bytes_accessed=legendre.size * 2 + 2**21,
            transcendentals=0,
        ),
        name="forward",
    )(harmonics, radial, legendre)


def table_kernel(cat_ref, sat_ref, cbt_ref, sbt_ref, flip_ref):
    wide = cbt_ref.shape[1]
    for a in range(cat_ref.shape[1]):
        flip_ref[:, a * wide : (a + 1) * wide] = (
            cat_ref[:, a : a + 1] * cbt_ref[...] - sat_ref[:, a : a + 1] * sbt_ref[...]
        ).astype(BF16)


def angle(index, period):
    phase = (index % period).astype(F32) * (2.0 * math.pi / period)
    return jnp.cos(phase), jnp.sin(phase)


def table_orders(order_table):
    grouped = order_table.reshape(-1, 1, 4)
    rows = jnp.broadcast_to(grouped, (grouped.shape[0], 2, 4)).reshape(-1)
    quarter = jnp.broadcast_to(
        jnp.arange(2, dtype=jnp.int32)[None, :, None], (grouped.shape[0], 2, 4)
    ).reshape(-1)
    return rows, quarter


def tables(order_table, pixels):
    rows, quarter = table_orders(order_table)
    low, wide = 64, 128
    shift = quarter * (pixels // 4)
    ca, sa = angle(jnp.arange(pixels // low, dtype=jnp.int32)[:, None] * low * rows[None], pixels)
    cb, sb = angle(jnp.arange(low, dtype=jnp.int32)[:, None] * rows[None] + shift[None], pixels)
    cat, sat = angle(rows[:, None] * (jnp.arange(pixels // wide, dtype=jnp.int32) * wide)[None], pixels)
    cbt, sbt = angle(
        rows[:, None] * jnp.arange(wide, dtype=jnp.int32)[None] + shift[:, None], pixels
    )
    count = rows.shape[0]
    flipped = pl.pallas_call(
        table_kernel,
        out_shape=jax.ShapeDtypeStruct((count, pixels), BF16),
        compiler_params=pltpu.CompilerParams(vmem_limit_bytes=24 * 2**20),
        cost_estimate=pl.CostEstimate(
            flops=3 * pixels * count, bytes_accessed=2 * pixels * count, transcendentals=0
        ),
        name="tables",
    )(cat, sat, cbt, sbt)
    return (ca, sa), (cb, sb), flipped


def rotation(order_table, pixels):
    rows, quarter = table_orders(order_table)
    sign = (2 * quarter - 1).astype(F32)
    columns = []
    for parity in range(2):
        cosine, sine = angle(rows * (2 - parity), 2 * pixels)
        columns += [cosine, sign * sine]
    return jnp.stack(columns, 1)


def cell_kernel(
    in_ref, ca_ref, sa_ref, cb_ref, sb_ref, analysis_ref, turn_ref, parity_ref, out_ref, products, synth, analysis, sem, *, block
):
    count, pixels = analysis_ref.shape
    fetch_analysis = pltpu.make_async_copy(analysis_ref, analysis, sem)
    fetch_analysis.start()
    low = cb_ref.shape[0]
    groups = in_ref.shape[1]
    step = products.shape[1] // (2 * LANES)
    width = step * LANES
    odd = jnp.broadcast_to(parity_ref[...], (count, LANES)) > 0.5
    turn = [jnp.broadcast_to(turn_ref[:, i : i + 1], (count, LANES)) for i in range(4)]
    rot_cos = jnp.where(odd, turn[2], turn[0])
    rot_sin = jnp.where(odd, turn[3], turn[1])
    scale = 1.0 / (128.0 * 64.0)
    back_cos = rot_cos * scale
    back_sin = rot_sin * scale

    def swap(x):
        return pltpu.roll(x.reshape(count // 8, 8, LANES), 4, 1).reshape(count, LANES)

    for first in range(0, groups, step):
        turned = [[], []]
        for g in range(first, first + step):
            arrived = in_ref[:, g].astype(F32)
            for f in range(2):
                x = arrived[:, f * 8 : (f + 1) * 8, :].reshape(count, LANES)
                turned[f].append((rot_cos * x + rot_sin * swap(x)).astype(BF16))
        turned = jnp.concatenate(turned[0] + turned[1], 1)
        for j in range(0, pixels, block):
            if first == 0:
                for a in range(j // low, (j + block) // low):
                    synth[a * low : (a + 1) * low, :] = (
                        ca_ref[a : a + 1, :] * cb_ref[...] - sa_ref[a : a + 1, :] * sb_ref[...]
                    ).astype(BF16)
            fields = jnp.dot(synth[j : j + block, :], turned, preferred_element_type=F32)
            alpha, beta = fields[:, :width], fields[:, width:]
            products[j : j + block, :width] = (beta * beta).astype(BF16)
            products[j : j + block, width:] = (alpha * beta).astype(BF16)
        if first == 0:
            fetch_analysis.wait()
        spectra = jnp.dot(analysis[...], products[...], preferred_element_type=F32)
        for g in range(step):
            parts = []
            for p in range(2):
                at = p * width + g * LANES
                x = spectra[:, at : at + LANES]
                parts.append((back_cos * x - back_sin * swap(x)).reshape(count // 8, 8, LANES))
            out_ref[first + g] = jnp.concatenate(parts, 1).astype(BF16)


def cells(arrived, high, low, analysis, turn, parity, step=4, block=1024):
    owners, groups, rows, lanes = arrived.shape
    count, pixels = analysis.shape
    whole = pl.BlockSpec(memory_space=pltpu.VMEM)
    anywhere = pl.BlockSpec(memory_space=pltpu.HBM)
    return pl.pallas_call(
        functools.partial(cell_kernel, block=block),
        in_specs=[*[whole] * 5, anywhere, whole, whole],
        out_specs=whole,
        out_shape=jax.ShapeDtypeStruct((groups, owners, rows, lanes), BF16),
        scratch_shapes=[
            pltpu.VMEM((pixels, 2 * step * lanes), BF16),
            pltpu.VMEM((pixels, count), BF16),
            pltpu.VMEM((count, pixels), BF16),
            pltpu.SemaphoreType.DMA,
        ],
        compiler_params=pltpu.CompilerParams(vmem_limit_bytes=50 * 2**20),
        cost_estimate=pl.CostEstimate(
            flops=2 * 2 * pixels * count * groups * 2 * lanes,
            bytes_accessed=4 * pixels * count + 2**22,
            transcendentals=0,
        ),
        name="cells",
    )(arrived, *high, *low, analysis, turn, parity)


def backward_kernel(
    place_ref, in_ref, near_ref, far_ref, leg_ref, out_ref, staged, profile, leg, sems
):
    step = pl.program_id(0)
    orders_dev, degrees = leg_ref.shape[:2]
    sources, cells_in = in_ref.shape[:2]
    chunks = staged.shape[0]
    per = cells_in // chunks
    rows = sources * per

    def fetch(o):
        return pltpu.make_async_copy(leg_ref.at[o], leg.at[o], sems.at[o])

    @pl.when(step == 0)
    def _():
        for o in range(orders_dev):
            fetch(o).start()

        def chunk(lane, carry):
            blocks = deal_blocks(
                [
                    in_ref[:, lane * per + i].astype(F32).reshape(sources * 16, LANES)
                    for i in range(per)
                ]
            )
            blocks = [shift_blocks(block, -i % per) for i, block in enumerate(blocks)]
            for i in range(per):
                for group in range(sources):
                    staged[lane, pl.ds((group * per + i) * 16, 16), :] = blocks[i][
                        group * 16 : (group + 1) * 16
                    ]
            return carry

        lax.fori_loop(0, chunks, chunk, 0)
        first = lax.broadcasted_iota(jnp.int32, (8, degrees), 0) < 4
        for z, ref in enumerate((near_ref, far_ref)):
            for x in range(ref.shape[0]):
                group = (place_ref[0] ^ z) * 4 + (place_ref[1] ^ x)
                for p in range(2):
                    lines = [
                        jnp.broadcast_to(ref[x, n, p : p + 1, :], (8, degrees)) for n in range(2)
                    ]
                    profile[p, group] = jnp.where(first, lines[0], lines[1])

    @pl.when(step > 0)
    def _():
        o = step - 1
        taken = jnp.concatenate(
            [
                jnp.concatenate(
                    [
                        staged[lane, pl.ds(p * 8 + part * 4 + o, rows, stride=16), :].astype(BF16)
                        for lane in range(chunks)
                    ],
                    1,
                )
                for part in range(2)
                for p in range(2)
            ],
            0,
        )
        fetch(o).wait()
        moments = lax.dot_general(
            taken, leg[o], (((1,), (1,)), ((), ())), preferred_element_type=F32
        )
        moments = moments.reshape(2, 2, sources, 8, degrees)
        for part in range(2):
            total = jnp.sum(moments[part] * profile[...], (0, 1))
            out_ref[0, :, part, :] = total[:4] + total[4:]


def backward(place, at_orders, profiles, legendre):
    sources = at_orders.shape[0]
    orders_dev, degrees, cycles = legendre.shape
    near = profiles[0].shape
    return pl.pallas_call(
        backward_kernel,
        grid_spec=pltpu.PrefetchScalarGridSpec(
            num_scalar_prefetch=1,
            grid=(orders_dev + 1,),
            in_specs=[
                pl.BlockSpec(at_orders.shape, lambda o, place: (0, 0, 0, 0)),
                *[pl.BlockSpec(near, lambda o, place: (0, 0, 0, 0))] * 2,
                pl.BlockSpec(memory_space=pltpu.HBM),
            ],
            out_specs=pl.BlockSpec(
                (1, 4, 2, degrees), lambda o, place: (jnp.maximum(o - 1, 0), 0, 0, 0)
            ),
            scratch_shapes=[
                pltpu.VMEM((cycles // LANES, sources * 8 * 16, LANES), F32),
                pltpu.VMEM((2, sources, 8, degrees), F32),
                pltpu.VMEM(legendre.shape, BF16),
                pltpu.SemaphoreType.DMA((orders_dev,)),
            ],
        ),
        out_shape=jax.ShapeDtypeStruct((orders_dev, 4, 2, degrees), F32),
        compiler_params=pltpu.CompilerParams(vmem_limit_bytes=52 * 2**20),
        cost_estimate=pl.CostEstimate(
            flops=2 * orders_dev * 256 * degrees * cycles,
            bytes_accessed=legendre.size * 2 + 2**21,
            transcendentals=0,
        ),
        name="backward",
    )(place, at_orders, *profiles, legendre)


def swapped(value, bit):
    return lax.ppermute(value, "node", [(i, i ^ bit) for i in range(lax.axis_size("node"))])


def on_device(harmonics, radial, node_weight, legendre, order_table, cycle_table):
    pixels = 4 * NSIDE
    groups = lax.axis_size("node")
    owners = lax.axis_size("sht")
    outgoing = forward(harmonics, radial, legendre)
    outgoing, radial, node_weight, order_table, cycle_table = lax.optimization_barrier(
        (outgoing, radial, node_weight, order_table, cycle_table)
    )
    arrived = lax.all_to_all(outgoing, "sht", 0, 0, tiled=True)
    parity = jnp.tile(((cycle_table - NSIDE + 1) % 2).astype(F32), 8)[None]
    turn = rotation(order_table, pixels)
    high, low, analysis = tables(order_table, pixels)
    radial, analysis = lax.optimization_barrier((radial, analysis))
    profile = radial * node_weight[:, None, None] * jnp.array([2.0, 4.0], F32)[None, :, None]
    near = jnp.stack([profile] + [swapped(profile, bit) for bit in (1, 2, 3)])
    far = swapped(near, 4)
    returning = cells(arrived, high, low, analysis, turn, parity)
    returning, far = lax.optimization_barrier((returning, far))
    returning = returning.reshape(groups * owners, 16, LANES)
    at_orders = lax.all_to_all(returning, ("node", "sht"), 0, 0, tiled=True)
    at_orders = at_orders.reshape(groups, owners, 16, LANES)
    node = lax.axis_index("node").astype(jnp.int32)
    place = jnp.stack([node // 4, node % 4])
    return backward(place, at_orders, (near, far), legendre)


def solution(mesh):
    in_specs = (
        P("sht", None, None, None),
        P("node", None, None),
        P("node"),
        P("sht", None, None),
        P(),
        P("sht"),
    )
    out_specs = P("sht", "node", None, None)
    return jax.shard_map(
        on_device, mesh=mesh, in_specs=in_specs, out_specs=out_specs, check_vma=False
    )
```

```python
import functools
import math

import jax
import jax.numpy as jnp
from jax import lax
from jax.experimental import pallas as pl
from jax.experimental.pallas import tpu as pltpu
from jax.sharding import PartitionSpec as P

NSIDE = 1024
F32 = jnp.float32
BF16 = jnp.bfloat16
LANES = 128


def deal_blocks(arrays):
    arrays = [arrays[-i % 8] for i in range(8)]
    block = lax.broadcasted_iota(jnp.int32, arrays[0].shape, 1) // 16
    for bit in (1, 2, 4):
        moved = block & bit != 0
        arrays = [jnp.where(moved, arrays[(i - bit) % 8], arrays[i]) for i in range(8)]
    return arrays


def shift_blocks(value, count):
    return value if count == 0 else pltpu.roll(value, 16 * count, 1)


def forward_kernel(harm_ref, radial_ref, leg_ref, out_ref, lines, staged):
    order = pl.program_id(0)
    samples, degrees = harm_ref.shape[1], harm_ref.shape[3]
    nodes = radial_ref.shape[0]
    groups = samples // 4
    chunks = degrees // LANES
    held = harm_ref[0].astype(F32).reshape(samples * 2, degrees)
    for lane in range(chunks):
        lines[lane] = held[:, lane * LANES : (lane + 1) * LANES]
    weighted = []
    for part in range(2):
        own = jnp.concatenate(
            [
                jnp.concatenate(
                    [
                        lines[lane, pl.ds(s * 2 + part, groups, stride=8), :]
                        for lane in range(chunks)
                    ],
                    1,
                )
                for s in range(4)
            ],
            0,
        )
        for f in range(2):
            for n in range(nodes):
                weighted.append((own * radial_ref[n, f : f + 1, :]).astype(BF16))
    coefficients = jnp.dot(
        jnp.concatenate(weighted, 0), leg_ref[0], preferred_element_type=F32
    )
    rows = nodes * samples
    for o in range(4):

        @pl.when(order == o)
        def _():
            for part in range(2):
                for f in range(2):
                    at = (part * 2 + f) * rows
                    for lane in range(staged.shape[0]):
                        staged[lane, pl.ds(f * 8 + part * 4 + o, rows, stride=16), :] = (
                            coefficients[at : at + rows, lane * LANES : (lane + 1) * LANES]
                        )

    @pl.when(order == 3)
    def _():
        size = groups * 16
        for lane in range(staged.shape[0]):
            blocks = deal_blocks(
                [shift_blocks(staged[lane, i * size : (i + 1) * size, :], i) for i in range(8)]
            )
            for i in range(8):
                out_ref[lane * 8 + i] = blocks[i].astype(BF16).reshape(groups, 16, LANES)


def forward(harmonics, radial, legendre):
    orders_dev, samples, _, degrees = harmonics.shape
    nodes = radial.shape[0]
    cycles = legendre.shape[2]
    out = (cycles // LANES * nodes * 4, samples // 4, 16, LANES)
    return pl.pallas_call(
        forward_kernel,
        grid=(orders_dev,),
        in_specs=[
            pl.BlockSpec((1, samples, 2, degrees), lambda o: (o, 0, 0, 0)),
            pl.BlockSpec(radial.shape, lambda o: (0, 0, 0)),
            pl.BlockSpec((1, degrees, cycles), lambda o: (o, 0, 0)),
        ],
        out_specs=pl.BlockSpec(out, lambda o: (0, 0, 0, 0)),
        scratch_shapes=[
            pltpu.VMEM((degrees // LANES, samples * 2, LANES), F32),
            pltpu.VMEM((cycles // LANES, nodes * samples * 16, LANES), F32),
        ],
        out_shape=jax.ShapeDtypeStruct(out, BF16),
        compiler_params=pltpu.CompilerParams(vmem_limit_bytes=58 * 2**20),
        cost_estimate=pl.CostEstimate(
            flops=2 * orders_dev * 256 * degrees * cycles,
            bytes_accessed=legendre.size * 2 + 2**21,
            transcendentals=0,
        ),
        name="forward",
    )(harmonics, radial, legendre)


def table_kernel(
    ca_ref, sa_ref, cb_ref, sb_ref, cat_ref, sat_ref, cbt_ref, sbt_ref, out_ref, flip_ref, flip, sems
):
    wide = cbt_ref.shape[1]
    pieces = sems.shape[0]
    per = cat_ref.shape[1] // pieces
    copies = []
    for piece in range(pieces):
        for a in range(piece * per, (piece + 1) * per):
            flip[:, a * wide : (a + 1) * wide] = (
                cat_ref[:, a : a + 1] * cbt_ref[...] - sat_ref[:, a : a + 1] * sbt_ref[...]
            ).astype(BF16)
        columns = pl.ds(piece * per * wide, per * wide)
        copies.append(
            pltpu.make_async_copy(flip.at[:, columns], flip_ref.at[:, columns], sems.at[piece])
        )
        copies[-1].start()
    low = cb_ref.shape[0]
    for a in range(ca_ref.shape[0]):
        out_ref[a * low : (a + 1) * low, :] = (
            ca_ref[a : a + 1, :] * cb_ref[...] - sa_ref[a : a + 1, :] * sb_ref[...]
        ).astype(BF16)
    for copy in copies:
        copy.wait()


def angle(index, period):
    phase = (index % period).astype(F32) * (2.0 * math.pi / period)
    return jnp.cos(phase), jnp.sin(phase)


def table_orders(order_table):
    grouped = order_table.reshape(-1, 1, 4)
    rows = jnp.broadcast_to(grouped, (grouped.shape[0], 2, 4)).reshape(-1)
    quarter = jnp.broadcast_to(
        jnp.arange(2, dtype=jnp.int32)[None, :, None], (grouped.shape[0], 2, 4)
    ).reshape(-1)
    return rows, quarter


def tables(order_table, pixels):
    rows, quarter = table_orders(order_table)
    low, wide = 64, 128
    shift = quarter * (pixels // 4)
    ca, sa = angle(jnp.arange(pixels // low, dtype=jnp.int32)[:, None] * low * rows[None], pixels)
    cb, sb = angle(jnp.arange(low, dtype=jnp.int32)[:, None] * rows[None] + shift[None], pixels)
    cat, sat = angle(rows[:, None] * (jnp.arange(pixels // wide, dtype=jnp.int32) * wide)[None], pixels)
    cbt, sbt = angle(
        rows[:, None] * jnp.arange(wide, dtype=jnp.int32)[None] + shift[:, None], pixels
    )
    count = rows.shape[0]
    return pl.pallas_call(
        table_kernel,
        out_specs=[pl.BlockSpec(memory_space=pltpu.VMEM), pl.BlockSpec(memory_space=pltpu.HBM)],
        out_shape=[
            jax.ShapeDtypeStruct((pixels, count), BF16),
            jax.ShapeDtypeStruct((count, pixels), BF16),
        ],
        scratch_shapes=[pltpu.VMEM((count, pixels), BF16), pltpu.SemaphoreType.DMA((2,))],
        compiler_params=pltpu.CompilerParams(vmem_limit_bytes=24 * 2**20),
        cost_estimate=pl.CostEstimate(
            flops=6 * pixels * count, bytes_accessed=4 * pixels * count, transcendentals=0
        ),
        name="tables",
    )(ca, sa, cb, sb, cat, sat, cbt, sbt)


def rotation(order_table, pixels):
    rows, quarter = table_orders(order_table)
    sign = (2 * quarter - 1).astype(F32)
    columns = []
    for parity in range(2):
        cosine, sine = angle(rows * (2 - parity), 2 * pixels)
        columns += [cosine, sign * sine]
    return jnp.stack(columns, 1)


def cell_kernel(
    in_ref, synth_ref, analysis_ref, turn_ref, parity_ref, out_ref, products, analysis, sem, *, block
):
    count, pixels = analysis_ref.shape
    fetch_analysis = pltpu.make_async_copy(analysis_ref, analysis, sem)
    fetch_analysis.start()
    groups = in_ref.shape[1]
    step = products.shape[1] // (2 * LANES)
    width = step * LANES
    odd = jnp.broadcast_to(parity_ref[...], (count, LANES)) > 0.5
    turn = [jnp.broadcast_to(turn_ref[:, i : i + 1], (count, LANES)) for i in range(4)]
    rot_cos = jnp.where(odd, turn[2], turn[0])
    rot_sin = jnp.where(odd, turn[3], turn[1])
    scale = 1.0 / (128.0 * 64.0)
    back_cos = rot_cos * scale
    back_sin = rot_sin * scale

    def swap(x):
        return pltpu.roll(x.reshape(count // 8, 8, LANES), 4, 1).reshape(count, LANES)

    for first in range(0, groups, step):
        turned = [[], []]
        for g in range(first, first + step):
            arrived = in_ref[:, g].astype(F32)
            for f in range(2):
                x = arrived[:, f * 8 : (f + 1) * 8, :].reshape(count, LANES)
                turned[f].append((rot_cos * x + rot_sin * swap(x)).astype(BF16))
        turned = jnp.concatenate(turned[0] + turned[1], 1)
        for j in range(0, pixels, block):
            fields = jnp.dot(synth_ref[j : j + block, :], turned, preferred_element_type=F32)
            alpha, beta = fields[:, :width], fields[:, width:]
            products[j : j + block, :width] = (beta * beta).astype(BF16)
            products[j : j + block, width:] = (alpha * beta).astype(BF16)
        if first == 0:
            fetch_analysis.wait()
        spectra = jnp.dot(analysis[...], products[...], preferred_element_type=F32)
        for g in range(step):
            parts = []
            for p in range(2):
                at = p * width + g * LANES
                x = spectra[:, at : at + LANES]
                parts.append((back_cos * x - back_sin * swap(x)).reshape(count // 8, 8, LANES))
            out_ref[first + g] = jnp.concatenate(parts, 1).astype(BF16)


def cells(arrived, synth, analysis, turn, parity, step=4, block=1024):
    owners, groups, rows, lanes = arrived.shape
    count, pixels = analysis.shape
    whole = pl.BlockSpec(memory_space=pltpu.VMEM)
    anywhere = pl.BlockSpec(memory_space=pltpu.HBM)
    return pl.pallas_call(
        functools.partial(cell_kernel, block=block),
        in_specs=[whole, whole, anywhere, whole, whole],
        out_specs=whole,
        out_shape=jax.ShapeDtypeStruct((groups, owners, rows, lanes), BF16),
        scratch_shapes=[
            pltpu.VMEM((pixels, 2 * step * lanes), BF16),
            pltpu.VMEM((count, pixels), BF16),
            pltpu.SemaphoreType.DMA,
        ],
        compiler_params=pltpu.CompilerParams(vmem_limit_bytes=48 * 2**20),
        cost_estimate=pl.CostEstimate(
            flops=2 * 2 * pixels * count * groups * 2 * lanes,
            bytes_accessed=4 * pixels * count + 2**22,
            transcendentals=0,
        ),
        name="cells",
    )(arrived, synth, analysis, turn, parity)


def backward_kernel(
    place_ref, in_ref, near_ref, far_ref, leg_ref, out_ref, staged, profile, leg, sems
):
    step = pl.program_id(0)
    orders_dev, degrees = leg_ref.shape[:2]
    sources, cells_in = in_ref.shape[:2]
    chunks = staged.shape[0]
    per = cells_in // chunks
    rows = sources * per

    def fetch(o):
        return pltpu.make_async_copy(leg_ref.at[o], leg.at[o], sems.at[o])

    @pl.when(step == 0)
    def _():
        for o in range(orders_dev):
            fetch(o).start()

        def chunk(lane, carry):
            blocks = deal_blocks(
                [
                    in_ref[:, lane * per + i].astype(F32).reshape(sources * 16, LANES)
                    for i in range(per)
                ]
            )
            blocks = [shift_blocks(block, -i % per) for i, block in enumerate(blocks)]
            for i in range(per):
                for group in range(sources):
                    staged[lane, pl.ds((group * per + i) * 16, 16), :] = blocks[i][
                        group * 16 : (group + 1) * 16
                    ]
            return carry

        lax.fori_loop(0, chunks, chunk, 0)
        first = lax.broadcasted_iota(jnp.int32, (8, degrees), 0) < 4
        for z, ref in enumerate((near_ref, far_ref)):
            for x in range(ref.shape[0]):
                group = (place_ref[0] ^ z) * 4 + (place_ref[1] ^ x)
                for p in range(2):
                    lines = [
                        jnp.broadcast_to(ref[x, n, p : p + 1, :], (8, degrees)) for n in range(2)
                    ]
                    profile[p, group] = jnp.where(first, lines[0], lines[1])

    @pl.when(step > 0)
    def _():
        o = step - 1
        taken = jnp.concatenate(
            [
                jnp.concatenate(
                    [
                        staged[lane, pl.ds(p * 8 + part * 4 + o, rows, stride=16), :].astype(BF16)
                        for lane in range(chunks)
                    ],
                    1,
                )
                for part in range(2)
                for p in range(2)
            ],
            0,
        )
        fetch(o).wait()
        moments = lax.dot_general(
            taken, leg[o], (((1,), (1,)), ((), ())), preferred_element_type=F32
        )
        moments = moments.reshape(2, 2, sources, 8, degrees)
        for part in range(2):
            total = jnp.sum(moments[part] * profile[...], (0, 1))
            out_ref[0, :, part, :] = total[:4] + total[4:]


def backward(place, at_orders, profiles, legendre):
    sources = at_orders.shape[0]
    orders_dev, degrees, cycles = legendre.shape
    near = profiles[0].shape
    return pl.pallas_call(
        backward_kernel,
        grid_spec=pltpu.PrefetchScalarGridSpec(
            num_scalar_prefetch=1,
            grid=(orders_dev + 1,),
            in_specs=[
                pl.BlockSpec(at_orders.shape, lambda o, place: (0, 0, 0, 0)),
                *[pl.BlockSpec(near, lambda o, place: (0, 0, 0, 0))] * 2,
                pl.BlockSpec(memory_space=pltpu.HBM),
            ],
            out_specs=pl.BlockSpec(
                (1, 4, 2, degrees), lambda o, place: (jnp.maximum(o - 1, 0), 0, 0, 0)
            ),
            scratch_shapes=[
                pltpu.VMEM((cycles // LANES, sources * 8 * 16, LANES), F32),
                pltpu.VMEM((2, sources, 8, degrees), F32),
                pltpu.VMEM(legendre.shape, BF16),
                pltpu.SemaphoreType.DMA((orders_dev,)),
            ],
        ),
        out_shape=jax.ShapeDtypeStruct((orders_dev, 4, 2, degrees), F32),
        compiler_params=pltpu.CompilerParams(vmem_limit_bytes=52 * 2**20),
        cost_estimate=pl.CostEstimate(
            flops=2 * orders_dev * 256 * degrees * cycles,
            bytes_accessed=legendre.size * 2 + 2**21,
            transcendentals=0,
        ),
        name="backward",
    )(place, at_orders, *profiles, legendre)


def swapped(value, bit):
    return lax.ppermute(value, "node", [(i, i ^ bit) for i in range(lax.axis_size("node"))])


def on_device(harmonics, radial, node_weight, legendre, order_table, cycle_table):
    pixels = 4 * NSIDE
    groups = lax.axis_size("node")
    owners = lax.axis_size("sht")
    outgoing = forward(harmonics, radial, legendre)
    outgoing, radial, node_weight, order_table, cycle_table = lax.optimization_barrier(
        (outgoing, radial, node_weight, order_table, cycle_table)
    )
    arrived = lax.all_to_all(outgoing, "sht", 0, 0, tiled=True)
    parity = jnp.tile(((cycle_table - NSIDE + 1) % 2).astype(F32), 8)[None]
    turn = rotation(order_table, pixels)
    synth, analysis = tables(order_table, pixels)
    radial, analysis = lax.optimization_barrier((radial, analysis))
    profile = radial * node_weight[:, None, None] * jnp.array([2.0, 4.0], F32)[None, :, None]
    near = jnp.stack([profile] + [swapped(profile, bit) for bit in (1, 2, 3)])
    far = swapped(near, 4)
    returning = cells(arrived, synth, analysis, turn, parity)
    returning, far = lax.optimization_barrier((returning, far))
    returning = returning.reshape(groups * owners, 16, LANES)
    at_orders = lax.all_to_all(returning, ("node", "sht"), 0, 0, tiled=True)
    at_orders = at_orders.reshape(groups, owners, 16, LANES)
    node = lax.axis_index("node").astype(jnp.int32)
    place = jnp.stack([node // 4, node % 4])
    return backward(place, at_orders, (near, far), legendre)


def solution(mesh):
    in_specs = (
        P("sht", None, None, None),
        P("node", None, None),
        P("node"),
        P("sht", None, None),
        P(),
        P("sht"),
    )
    out_specs = P("sht", "node", None, None)
    return jax.shard_map(
        on_device, mesh=mesh, in_specs=in_specs, out_specs=out_specs, check_vma=False
    )
```

```python
import functools
import math

import jax
import jax.numpy as jnp
from jax import lax
from jax.experimental import pallas as pl
from jax.experimental.pallas import tpu as pltpu
from jax.sharding import PartitionSpec as P

NSIDE = 1024
F32 = jnp.float32
BF16 = jnp.bfloat16
LANES = 128


def deal_blocks(arrays):
    arrays = [arrays[-i % 8] for i in range(8)]
    block = lax.broadcasted_iota(jnp.int32, arrays[0].shape, 1) // 16
    for bit in (1, 2, 4):
        moved = block & bit != 0
        arrays = [jnp.where(moved, arrays[(i - bit) % 8], arrays[i]) for i in range(8)]
    return arrays


def shift_blocks(value, count):
    return value if count == 0 else pltpu.roll(value, 16 * count, 1)


def forward_kernel(harm_ref, radial_ref, leg_ref, out_ref, lines, staged, done, sems):
    order = pl.program_id(0)
    samples, degrees = harm_ref.shape[1], harm_ref.shape[3]
    nodes = radial_ref.shape[0]
    groups = samples // 4
    chunks = degrees // LANES
    held = harm_ref[0].astype(F32).reshape(samples * 2, degrees)
    for lane in range(chunks):
        lines[lane] = held[:, lane * LANES : (lane + 1) * LANES]
    weighted = []
    for part in range(2):
        own = jnp.concatenate(
            [
                jnp.concatenate(
                    [
                        lines[lane, pl.ds(s * 2 + part, groups, stride=8), :]
                        for lane in range(chunks)
                    ],
                    1,
                )
                for s in range(4)
            ],
            0,
        )
        for f in range(2):
            for n in range(nodes):
                weighted.append((own * radial_ref[n, f : f + 1, :]).astype(BF16))
    coefficients = jnp.dot(
        jnp.concatenate(weighted, 0), leg_ref[0], preferred_element_type=F32
    )
    rows = nodes * samples
    for o in range(4):

        @pl.when(order == o)
        def _():
            for part in range(2):
                for f in range(2):
                    at = (part * 2 + f) * rows
                    for lane in range(staged.shape[0]):
                        staged[lane, pl.ds(f * 8 + part * 4 + o, rows, stride=16), :] = (
                            coefficients[at : at + rows, lane * LANES : (lane + 1) * LANES]
                        )

    @pl.when(order == 3)
    def _():
        size = groups * 16
        copies = []
        for lane in range(staged.shape[0]):
            blocks = deal_blocks(
                [shift_blocks(staged[lane, i * size : (i + 1) * size, :], i) for i in range(8)]
            )
            for i in range(8):
                done[lane * 8 + i] = blocks[i].astype(BF16).reshape(groups, 16, LANES)
            piece = pl.ds(lane * 8, 8)
            copies.append(pltpu.make_async_copy(done.at[piece], out_ref.at[piece], sems.at[lane]))
            copies[-1].start()
        for copy in copies:
            copy.wait()


def forward(harmonics, radial, legendre):
    orders_dev, samples, _, degrees = harmonics.shape
    nodes = radial.shape[0]
    cycles = legendre.shape[2]
    out = (cycles // LANES * nodes * 4, samples // 4, 16, LANES)
    return pl.pallas_call(
        forward_kernel,
        grid=(orders_dev,),
        in_specs=[
            pl.BlockSpec((1, samples, 2, degrees), lambda o: (o, 0, 0, 0)),
            pl.BlockSpec(radial.shape, lambda o: (0, 0, 0)),
            pl.BlockSpec((1, degrees, cycles), lambda o: (o, 0, 0)),
        ],
        out_specs=pl.BlockSpec(memory_space=pltpu.HBM),
        scratch_shapes=[
            pltpu.VMEM((degrees // LANES, samples * 2, LANES), F32),
            pltpu.VMEM((cycles // LANES, nodes * samples * 16, LANES), F32),
            pltpu.VMEM(out, BF16),
            pltpu.SemaphoreType.DMA((cycles // LANES,)),
        ],
        out_shape=jax.ShapeDtypeStruct(out, BF16),
        compiler_params=pltpu.CompilerParams(vmem_limit_bytes=58 * 2**20),
        cost_estimate=pl.CostEstimate(
            flops=2 * orders_dev * 256 * degrees * cycles,
            bytes_accessed=legendre.size * 2 + 2**21,
            transcendentals=0,
        ),
        name="forward",
    )(harmonics, radial, legendre)


def table_kernel(
    ca_ref, sa_ref, cb_ref, sb_ref, cat_ref, sat_ref, cbt_ref, sbt_ref, out_ref, flip_ref, flip, sems
):
    wide = cbt_ref.shape[1]
    pieces = sems.shape[0]
    per = cat_ref.shape[1] // pieces
    copies = []
    for piece in range(pieces):
        for a in range(piece * per, (piece + 1) * per):
            flip[:, a * wide : (a + 1) * wide] = (
                cat_ref[:, a : a + 1] * cbt_ref[...] - sat_ref[:, a : a + 1] * sbt_ref[...]
            ).astype(BF16)
        columns = pl.ds(piece * per * wide, per * wide)
        copies.append(
            pltpu.make_async_copy(flip.at[:, columns], flip_ref.at[:, columns], sems.at[piece])
        )
        copies[-1].start()
    low = cb_ref.shape[0]
    for a in range(ca_ref.shape[0]):
        out_ref[a * low : (a + 1) * low, :] = (
            ca_ref[a : a + 1, :] * cb_ref[...] - sa_ref[a : a + 1, :] * sb_ref[...]
        ).astype(BF16)
    for copy in copies:
        copy.wait()


def angle(index, period):
    phase = (index % period).astype(F32) * (2.0 * math.pi / period)
    return jnp.cos(phase), jnp.sin(phase)


def table_orders(order_table):
    grouped = order_table.reshape(-1, 1, 4)
    rows = jnp.broadcast_to(grouped, (grouped.shape[0], 2, 4)).reshape(-1)
    quarter = jnp.broadcast_to(
        jnp.arange(2, dtype=jnp.int32)[None, :, None], (grouped.shape[0], 2, 4)
    ).reshape(-1)
    return rows, quarter


def tables(order_table, pixels):
    rows, quarter = table_orders(order_table)
    low, wide = 64, 128
    shift = quarter * (pixels // 4)
    ca, sa = angle(jnp.arange(pixels // low, dtype=jnp.int32)[:, None] * low * rows[None], pixels)
    cb, sb = angle(jnp.arange(low, dtype=jnp.int32)[:, None] * rows[None] + shift[None], pixels)
    cat, sat = angle(rows[:, None] * (jnp.arange(pixels // wide, dtype=jnp.int32) * wide)[None], pixels)
    cbt, sbt = angle(
        rows[:, None] * jnp.arange(wide, dtype=jnp.int32)[None] + shift[:, None], pixels
    )
    count = rows.shape[0]
    return pl.pallas_call(
        table_kernel,
        out_specs=[pl.BlockSpec(memory_space=pltpu.VMEM), pl.BlockSpec(memory_space=pltpu.HBM)],
        out_shape=[
            jax.ShapeDtypeStruct((pixels, count), BF16),
            jax.ShapeDtypeStruct((count, pixels), BF16),
        ],
        scratch_shapes=[pltpu.VMEM((count, pixels), BF16), pltpu.SemaphoreType.DMA((2,))],
        compiler_params=pltpu.CompilerParams(vmem_limit_bytes=24 * 2**20),
        cost_estimate=pl.CostEstimate(
            flops=6 * pixels * count, bytes_accessed=4 * pixels * count, transcendentals=0
        ),
        name="tables",
    )(ca, sa, cb, sb, cat, sat, cbt, sbt)


def rotation(order_table, pixels):
    rows, quarter = table_orders(order_table)
    sign = (2 * quarter - 1).astype(F32)
    columns = []
    for parity in range(2):
        cosine, sine = angle(rows * (2 - parity), 2 * pixels)
        columns += [cosine, sign * sine]
    return jnp.stack(columns, 1)


def cell_kernel(
    in_ref, synth_ref, analysis_ref, turn_ref, parity_ref, out_ref, products, analysis, sem, *, block
):
    count, pixels = analysis_ref.shape
    fetch_analysis = pltpu.make_async_copy(analysis_ref, analysis, sem)
    fetch_analysis.start()
    groups = in_ref.shape[1]
    step = products.shape[1] // (2 * LANES)
    width = step * LANES
    odd = jnp.broadcast_to(parity_ref[...], (count, LANES)) > 0.5
    turn = [jnp.broadcast_to(turn_ref[:, i : i + 1], (count, LANES)) for i in range(4)]
    rot_cos = jnp.where(odd, turn[2], turn[0])
    rot_sin = jnp.where(odd, turn[3], turn[1])
    scale = 1.0 / (128.0 * 64.0)
    back_cos = rot_cos * scale
    back_sin = rot_sin * scale

    def swap(x):
        return pltpu.roll(x.reshape(count // 8, 8, LANES), 4, 1).reshape(count, LANES)

    for first in range(0, groups, step):
        turned = [[], []]
        for g in range(first, first + step):
            arrived = in_ref[:, g].astype(F32)
            for f in range(2):
                x = arrived[:, f * 8 : (f + 1) * 8, :].reshape(count, LANES)
                turned[f].append((rot_cos * x + rot_sin * swap(x)).astype(BF16))
        turned = jnp.concatenate(turned[0] + turned[1], 1)
        for j in range(0, pixels, block):
            fields = jnp.dot(synth_ref[j : j + block, :], turned, preferred_element_type=F32)
            alpha, beta = fields[:, :width], fields[:, width:]
            products[j : j + block, :width] = (beta * beta).astype(BF16)
            products[j : j + block, width:] = (alpha * beta).astype(BF16)
        if first == 0:
            fetch_analysis.wait()
        spectra = jnp.dot(analysis[...], products[...], preferred_element_type=F32)
        for g in range(step):
            parts = []
            for p in range(2):
                at = p * width + g * LANES
                x = spectra[:, at : at + LANES]
                parts.append((back_cos * x - back_sin * swap(x)).reshape(count // 8, 8, LANES))
            out_ref[:, first + g] = jnp.concatenate(parts, 1).astype(BF16)


def cells(arrived, synth, analysis, turn, parity, step=4, block=1024):
    owners, groups, rows, lanes = arrived.shape
    count, pixels = analysis.shape
    whole = pl.BlockSpec(memory_space=pltpu.VMEM)
    anywhere = pl.BlockSpec(memory_space=pltpu.HBM)
    return pl.pallas_call(
        functools.partial(cell_kernel, block=block),
        in_specs=[whole, whole, anywhere, whole, whole],
        out_specs=whole,
        out_shape=jax.ShapeDtypeStruct((owners, groups, rows, lanes), BF16),
        scratch_shapes=[
            pltpu.VMEM((pixels, 2 * step * lanes), BF16),
            pltpu.VMEM((count, pixels), BF16),
            pltpu.SemaphoreType.DMA,
        ],
        compiler_params=pltpu.CompilerParams(vmem_limit_bytes=48 * 2**20),
        cost_estimate=pl.CostEstimate(
            flops=2 * 2 * pixels * count * groups * 2 * lanes,
            bytes_accessed=4 * pixels * count + 2**22,
            transcendentals=0,
        ),
        name="cells",
    )(arrived, synth, analysis, turn, parity)


def backward_kernel(
    place_ref, in_ref, near_ref, far_ref, leg_ref, out_ref, staged, profile, leg, sems
):
    step = pl.program_id(0)
    orders_dev, degrees = leg_ref.shape[:2]
    cells_in, sources = in_ref.shape[:2]
    chunks = staged.shape[0]
    per = cells_in // chunks
    rows = sources * per

    def fetch(o):
        return pltpu.make_async_copy(leg_ref.at[o], leg.at[o], sems.at[o])

    @pl.when(step == 0)
    def _():
        for o in range(orders_dev):
            fetch(o).start()

        def chunk(lane, carry):
            blocks = deal_blocks(
                [
                    in_ref[lane * per + i].astype(F32).reshape(sources * 16, LANES)
                    for i in range(per)
                ]
            )
            blocks = [shift_blocks(block, -i % per) for i, block in enumerate(blocks)]
            for i in range(per):
                for group in range(sources):
                    staged[lane, pl.ds((group * per + i) * 16, 16), :] = blocks[i][
                        group * 16 : (group + 1) * 16
                    ]
            return carry

        lax.fori_loop(0, chunks, chunk, 0)
        first = lax.broadcasted_iota(jnp.int32, (8, degrees), 0) < 4
        for z, ref in enumerate((near_ref, far_ref)):
            for x in range(ref.shape[0]):
                group = (place_ref[0] ^ z) * 4 + (place_ref[1] ^ x)
                for p in range(2):
                    lines = [
                        jnp.broadcast_to(ref[x, n, p : p + 1, :], (8, degrees)) for n in range(2)
                    ]
                    profile[p, group] = jnp.where(first, lines[0], lines[1])

    @pl.when(step > 0)
    def _():
        o = step - 1
        taken = jnp.concatenate(
            [
                jnp.concatenate(
                    [
                        staged[lane, pl.ds(p * 8 + part * 4 + o, rows, stride=16), :].astype(BF16)
                        for lane in range(chunks)
                    ],
                    1,
                )
                for part in range(2)
                for p in range(2)
            ],
            0,
        )
        fetch(o).wait()
        moments = lax.dot_general(
            taken, leg[o], (((1,), (1,)), ((), ())), preferred_element_type=F32
        )
        moments = moments.reshape(2, 2, sources, 8, degrees)
        for part in range(2):
            total = jnp.sum(moments[part] * profile[...], (0, 1))
            out_ref[0, :, part, :] = total[:4] + total[4:]


def backward(place, at_orders, profiles, legendre):
    sources = at_orders.shape[1]
    orders_dev, degrees, cycles = legendre.shape
    near = profiles[0].shape
    return pl.pallas_call(
        backward_kernel,
        grid_spec=pltpu.PrefetchScalarGridSpec(
            num_scalar_prefetch=1,
            grid=(orders_dev + 1,),
            in_specs=[
                pl.BlockSpec(at_orders.shape, lambda o, place: (0, 0, 0, 0)),
                *[pl.BlockSpec(near, lambda o, place: (0, 0, 0, 0))] * 2,
                pl.BlockSpec(memory_space=pltpu.HBM),
            ],
            out_specs=pl.BlockSpec(
                (1, 4, 2, degrees), lambda o, place: (jnp.maximum(o - 1, 0), 0, 0, 0)
            ),
            scratch_shapes=[
                pltpu.VMEM((cycles // LANES, sources * 8 * 16, LANES), F32),
                pltpu.VMEM((2, sources, 8, degrees), F32),
                pltpu.VMEM(legendre.shape, BF16),
                pltpu.SemaphoreType.DMA((orders_dev,)),
            ],
        ),
        out_shape=jax.ShapeDtypeStruct((orders_dev, 4, 2, degrees), F32),
        compiler_params=pltpu.CompilerParams(vmem_limit_bytes=52 * 2**20),
        cost_estimate=pl.CostEstimate(
            flops=2 * orders_dev * 256 * degrees * cycles,
            bytes_accessed=legendre.size * 2 + 2**21,
            transcendentals=0,
        ),
        name="backward",
    )(place, at_orders, *profiles, legendre)


def swapped(value, bit):
    return lax.ppermute(value, "node", [(i, i ^ bit) for i in range(lax.axis_size("node"))])


def on_device(harmonics, radial, node_weight, legendre, order_table, cycle_table):
    pixels = 4 * NSIDE
    groups = lax.axis_size("node")
    owners = lax.axis_size("sht")
    outgoing = forward(harmonics, radial, legendre)
    outgoing, radial, node_weight, order_table, cycle_table = lax.optimization_barrier(
        (outgoing, radial, node_weight, order_table, cycle_table)
    )
    arrived = lax.all_to_all(outgoing, "sht", 0, 0, tiled=True)
    parity = jnp.tile(((cycle_table - NSIDE + 1) % 2).astype(F32), 8)[None]
    turn = rotation(order_table, pixels)
    synth, analysis = tables(order_table, pixels)
    radial, analysis = lax.optimization_barrier((radial, analysis))
    profile = radial * node_weight[:, None, None] * jnp.array([2.0, 4.0], F32)[None, :, None]
    near = jnp.stack([profile] + [swapped(profile, bit) for bit in (1, 2, 3)])
    far = swapped(near, 4)
    returning = cells(arrived, synth, analysis, turn, parity)
    returning, far = lax.optimization_barrier((returning, far))
    returning = returning.reshape(owners * groups, 16, LANES)
    at_orders = lax.all_to_all(returning, ("sht", "node"), 0, 0, tiled=True)
    at_orders = at_orders.reshape(owners, groups, 16, LANES)
    node = lax.axis_index("node").astype(jnp.int32)
    place = jnp.stack([node // 4, node % 4])
    return backward(place, at_orders, (near, far), legendre)


def solution(mesh):
    in_specs = (
        P("sht", None, None, None),
        P("node", None, None),
        P("node"),
        P("sht", None, None),
        P(),
        P("sht"),
    )
    out_specs = P("sht", "node", None, None)
    return jax.shard_map(
        on_device, mesh=mesh, in_specs=in_specs, out_specs=out_specs, check_vma=False
    )
```

```python
import functools
import math

import jax
import jax.numpy as jnp
from jax import lax
from jax.experimental import pallas as pl
from jax.experimental.pallas import tpu as pltpu
from jax.sharding import PartitionSpec as P

NSIDE = 1024
F32 = jnp.float32
BF16 = jnp.bfloat16
LANES = 128


def deal_blocks(arrays):
    arrays = [arrays[-i % 8] for i in range(8)]
    block = lax.broadcasted_iota(jnp.int32, arrays[0].shape, 1) // 16
    for bit in (1, 2, 4):
        moved = block & bit != 0
        arrays = [jnp.where(moved, arrays[(i - bit) % 8], arrays[i]) for i in range(8)]
    return arrays


def shift_blocks(value, count):
    return value if count == 0 else pltpu.roll(value, 16 * count, 1)


def forward_kernel(harm_ref, radial_ref, leg_ref, out_ref, lines, staged, done, sems):
    order = pl.program_id(0)
    samples, degrees = harm_ref.shape[1], harm_ref.shape[3]
    nodes = radial_ref.shape[0]
    groups = samples // 4
    chunks = degrees // LANES
    held = harm_ref[0].astype(F32).reshape(samples * 2, degrees)
    for lane in range(chunks):
        lines[lane] = held[:, lane * LANES : (lane + 1) * LANES]
    weighted = []
    for part in range(2):
        own = jnp.concatenate(
            [
                jnp.concatenate(
                    [
                        lines[lane, pl.ds(s * 2 + part, groups, stride=8), :]
                        for lane in range(chunks)
                    ],
                    1,
                )
                for s in range(4)
            ],
            0,
        )
        for f in range(2):
            for n in range(nodes):
                weighted.append((own * radial_ref[n, f : f + 1, :]).astype(BF16))
    coefficients = jnp.dot(
        jnp.concatenate(weighted, 0), leg_ref[0], preferred_element_type=F32
    )
    rows = nodes * samples
    for o in range(4):

        @pl.when(order == o)
        def _():
            for part in range(2):
                for f in range(2):
                    at = (part * 2 + f) * rows
                    for lane in range(staged.shape[0]):
                        staged[lane, pl.ds(f * 8 + part * 4 + o, rows, stride=16), :] = (
                            coefficients[at : at + rows, lane * LANES : (lane + 1) * LANES]
                        )

    @pl.when(order == 3)
    def _():
        size = groups * 16
        copies = []
        for lane in range(staged.shape[0]):
            blocks = deal_blocks(
                [shift_blocks(staged[lane, i * size : (i + 1) * size, :], i) for i in range(8)]
            )
            for i in range(8):
                done[lane * 8 + i] = blocks[i].astype(BF16).reshape(groups, 16, LANES)
            piece = pl.ds(lane * 8, 8)
            copies.append(pltpu.make_async_copy(done.at[piece], out_ref.at[piece], sems.at[lane]))
            copies[-1].start()
        for copy in copies:
            copy.wait()


def forward(harmonics, radial, legendre):
    orders_dev, samples, _, degrees = harmonics.shape
    nodes = radial.shape[0]
    cycles = legendre.shape[2]
    out = (cycles // LANES * nodes * 4, samples // 4, 16, LANES)
    return pl.pallas_call(
        forward_kernel,
        grid=(orders_dev,),
        in_specs=[
            pl.BlockSpec((1, samples, 2, degrees), lambda o: (o, 0, 0, 0)),
            pl.BlockSpec(radial.shape, lambda o: (0, 0, 0)),
            pl.BlockSpec((1, degrees, cycles), lambda o: (o, 0, 0)),
        ],
        out_specs=pl.BlockSpec(memory_space=pltpu.HBM),
        scratch_shapes=[
            pltpu.VMEM((degrees // LANES, samples * 2, LANES), F32),
            pltpu.VMEM((cycles // LANES, nodes * samples * 16, LANES), F32),
            pltpu.VMEM(out, BF16),
            pltpu.SemaphoreType.DMA((cycles // LANES,)),
        ],
        out_shape=jax.ShapeDtypeStruct(out, BF16),
        compiler_params=pltpu.CompilerParams(vmem_limit_bytes=58 * 2**20),
        cost_estimate=pl.CostEstimate(
            flops=2 * orders_dev * 256 * degrees * cycles,
            bytes_accessed=legendre.size * 2 + 2**21,
            transcendentals=0,
        ),
        name="forward",
    )(harmonics, radial, legendre)


def table_kernel(
    ca_ref, sa_ref, cb_ref, sb_ref, cat_ref, sat_ref, cbt_ref, sbt_ref, out_ref, flip_ref, flip, sems
):
    wide = cbt_ref.shape[1]
    pieces = sems.shape[0]
    per = cat_ref.shape[1] // pieces
    copies = []
    for piece in range(pieces):
        for a in range(piece * per, (piece + 1) * per):
            flip[:, a * wide : (a + 1) * wide] = (
                cat_ref[:, a : a + 1] * cbt_ref[...] - sat_ref[:, a : a + 1] * sbt_ref[...]
            ).astype(BF16)
        columns = pl.ds(piece * per * wide, per * wide)
        copies.append(
            pltpu.make_async_copy(flip.at[:, columns], flip_ref.at[:, columns], sems.at[piece])
        )
        copies[-1].start()
    low = cb_ref.shape[0]
    for a in range(ca_ref.shape[0]):
        out_ref[a * low : (a + 1) * low, :] = (
            ca_ref[a : a + 1, :] * cb_ref[...] - sa_ref[a : a + 1, :] * sb_ref[...]
        ).astype(BF16)
    for copy in copies:
        copy.wait()


def angle(index, period):
    phase = (index % period).astype(F32) * (2.0 * math.pi / period)
    return jnp.cos(phase), jnp.sin(phase)


def table_orders(order_table):
    grouped = order_table.reshape(-1, 1, 4)
    rows = jnp.broadcast_to(grouped, (grouped.shape[0], 2, 4)).reshape(-1)
    quarter = jnp.broadcast_to(
        jnp.arange(2, dtype=jnp.int32)[None, :, None], (grouped.shape[0], 2, 4)
    ).reshape(-1)
    return rows, quarter


def tables(order_table, pixels):
    rows, quarter = table_orders(order_table)
    low, wide = 64, 128
    shift = quarter * (pixels // 4)
    ca, sa = angle(jnp.arange(pixels // low, dtype=jnp.int32)[:, None] * low * rows[None], pixels)
    cb, sb = angle(jnp.arange(low, dtype=jnp.int32)[:, None] * rows[None] + shift[None], pixels)
    cat, sat = angle(rows[:, None] * (jnp.arange(pixels // wide, dtype=jnp.int32) * wide)[None], pixels)
    cbt, sbt = angle(
        rows[:, None] * jnp.arange(wide, dtype=jnp.int32)[None] + shift[:, None], pixels
    )
    count = rows.shape[0]
    return pl.pallas_call(
        table_kernel,
        out_specs=[pl.BlockSpec(memory_space=pltpu.VMEM), pl.BlockSpec(memory_space=pltpu.HBM)],
        out_shape=[
            jax.ShapeDtypeStruct((pixels, count), BF16),
            jax.ShapeDtypeStruct((count, pixels), BF16),
        ],
        scratch_shapes=[pltpu.VMEM((count, pixels), BF16), pltpu.SemaphoreType.DMA((2,))],
        compiler_params=pltpu.CompilerParams(vmem_limit_bytes=24 * 2**20),
        cost_estimate=pl.CostEstimate(
            flops=6 * pixels * count, bytes_accessed=4 * pixels * count, transcendentals=0
        ),
        name="tables",
    )(ca, sa, cb, sb, cat, sat, cbt, sbt)


def rotation(order_table, pixels):
    rows, quarter = table_orders(order_table)
    sign = (2 * quarter - 1).astype(F32)
    columns = []
    for parity in range(2):
        cosine, sine = angle(rows * (2 - parity), 2 * pixels)
        columns += [cosine, sign * sine]
    return jnp.stack(columns, 1)


def cell_kernel(
    in_ref, synth_ref, analysis_ref, turn_ref, parity_ref, out_ref, products, analysis, sem, done, out_sems, *, block
):
    count, pixels = analysis_ref.shape
    fetch_analysis = pltpu.make_async_copy(analysis_ref, analysis, sem)
    fetch_analysis.start()
    groups = in_ref.shape[1]
    step = products.shape[1] // (2 * LANES)
    width = step * LANES
    odd = jnp.broadcast_to(parity_ref[...], (count, LANES)) > 0.5
    turn = [jnp.broadcast_to(turn_ref[:, i : i + 1], (count, LANES)) for i in range(4)]
    rot_cos = jnp.where(odd, turn[2], turn[0])
    rot_sin = jnp.where(odd, turn[3], turn[1])
    scale = 1.0 / (128.0 * 64.0)
    back_cos = rot_cos * scale
    back_sin = rot_sin * scale

    def swap(x):
        return pltpu.roll(x.reshape(count // 8, 8, LANES), 4, 1).reshape(count, LANES)

    copies = []
    for first in range(0, groups, step):
        turned = [[], []]
        for g in range(first, first + step):
            arrived = in_ref[:, g].astype(F32)
            for f in range(2):
                x = arrived[:, f * 8 : (f + 1) * 8, :].reshape(count, LANES)
                turned[f].append((rot_cos * x + rot_sin * swap(x)).astype(BF16))
        turned = jnp.concatenate(turned[0] + turned[1], 1)
        for j in range(0, pixels, block):
            fields = jnp.dot(synth_ref[j : j + block, :], turned, preferred_element_type=F32)
            alpha, beta = fields[:, :width], fields[:, width:]
            products[j : j + block, :width] = (beta * beta).astype(BF16)
            products[j : j + block, width:] = (alpha * beta).astype(BF16)
        if first == 0:
            fetch_analysis.wait()
        spectra = jnp.dot(analysis[...], products[...], preferred_element_type=F32)
        for g in range(step):
            parts = []
            for p in range(2):
                at = p * width + g * LANES
                x = spectra[:, at : at + LANES]
                parts.append((back_cos * x - back_sin * swap(x)).reshape(count // 8, 8, LANES))
            done[:, first + g] = jnp.concatenate(parts, 1).astype(BF16)
        piece = pl.ds(first, step)
        copies.append(
            pltpu.make_async_copy(
                done.at[:, piece], out_ref.at[:, piece], out_sems.at[first // step]
            )
        )
        copies[-1].start()
    for copy in copies:
        copy.wait()


def cells(arrived, synth, analysis, turn, parity, step=2, block=1024):
    owners, groups, rows, lanes = arrived.shape
    count, pixels = analysis.shape
    whole = pl.BlockSpec(memory_space=pltpu.VMEM)
    anywhere = pl.BlockSpec(memory_space=pltpu.HBM)
    return pl.pallas_call(
        functools.partial(cell_kernel, block=block),
        in_specs=[whole, whole, anywhere, whole, whole],
        out_specs=anywhere,
        out_shape=jax.ShapeDtypeStruct((owners, groups, rows, lanes), BF16),
        scratch_shapes=[
            pltpu.VMEM((pixels, 2 * step * lanes), BF16),
            pltpu.VMEM((count, pixels), BF16),
            pltpu.SemaphoreType.DMA,
            pltpu.VMEM(arrived.shape, BF16),
            pltpu.SemaphoreType.DMA((groups // step,)),
        ],
        compiler_params=pltpu.CompilerParams(vmem_limit_bytes=48 * 2**20),
        cost_estimate=pl.CostEstimate(
            flops=2 * 2 * pixels * count * groups * 2 * lanes,
            bytes_accessed=4 * pixels * count + 2**22,
            transcendentals=0,
        ),
        name="cells",
    )(arrived, synth, analysis, turn, parity)


def backward_kernel(
    place_ref, in_ref, near_ref, far_ref, leg_ref, out_ref, staged, profile, leg, sems
):
    step = pl.program_id(0)
    orders_dev, degrees = leg_ref.shape[:2]
    cells_in, sources = in_ref.shape[:2]
    chunks = staged.shape[0]
    per = cells_in // chunks
    rows = sources * per

    def fetch(o):
        return pltpu.make_async_copy(leg_ref.at[o], leg.at[o], sems.at[o])

    @pl.when(step == 0)
    def _():
        for o in range(orders_dev):
            fetch(o).start()

        def chunk(lane, carry):
            blocks = deal_blocks(
                [
                    in_ref[lane * per + i].astype(F32).reshape(sources * 16, LANES)
                    for i in range(per)
                ]
            )
            blocks = [shift_blocks(block, -i % per) for i, block in enumerate(blocks)]
            for i in range(per):
                for group in range(sources):
                    staged[lane, pl.ds((group * per + i) * 16, 16), :] = blocks[i][
                        group * 16 : (group + 1) * 16
                    ]
            return carry

        lax.fori_loop(0, chunks, chunk, 0)
        first = lax.broadcasted_iota(jnp.int32, (8, degrees), 0) < 4
        for z, ref in enumerate((near_ref, far_ref)):
            for x in range(ref.shape[0]):
                group = (place_ref[0] ^ z) * 4 + (place_ref[1] ^ x)
                for p in range(2):
                    lines = [
                        jnp.broadcast_to(ref[x, n, p : p + 1, :], (8, degrees)) for n in range(2)
                    ]
                    profile[p, group] = jnp.where(first, lines[0], lines[1])

    @pl.when(step > 0)
    def _():
        o = step - 1
        taken = jnp.concatenate(
            [
                jnp.concatenate(
                    [
                        staged[lane, pl.ds(p * 8 + part * 4 + o, rows, stride=16), :].astype(BF16)
                        for lane in range(chunks)
                    ],
                    1,
                )
                for part in range(2)
                for p in range(2)
            ],
            0,
        )
        fetch(o).wait()
        moments = lax.dot_general(
            taken, leg[o], (((1,), (1,)), ((), ())), preferred_element_type=F32
        )
        moments = moments.reshape(2, 2, sources, 8, degrees)
        for part in range(2):
            total = jnp.sum(moments[part] * profile[...], (0, 1))
            out_ref[0, :, part, :] = total[:4] + total[4:]


def backward(place, at_orders, profiles, legendre):
    sources = at_orders.shape[1]
    orders_dev, degrees, cycles = legendre.shape
    near = profiles[0].shape
    return pl.pallas_call(
        backward_kernel,
        grid_spec=pltpu.PrefetchScalarGridSpec(
            num_scalar_prefetch=1,
            grid=(orders_dev + 1,),
            in_specs=[
                pl.BlockSpec(at_orders.shape, lambda o, place: (0, 0, 0, 0)),
                *[pl.BlockSpec(near, lambda o, place: (0, 0, 0, 0))] * 2,
                pl.BlockSpec(memory_space=pltpu.HBM),
            ],
            out_specs=pl.BlockSpec(
                (1, 4, 2, degrees), lambda o, place: (jnp.maximum(o - 1, 0), 0, 0, 0)
            ),
            scratch_shapes=[
                pltpu.VMEM((cycles // LANES, sources * 8 * 16, LANES), F32),
                pltpu.VMEM((2, sources, 8, degrees), F32),
                pltpu.VMEM(legendre.shape, BF16),
                pltpu.SemaphoreType.DMA((orders_dev,)),
            ],
        ),
        out_shape=jax.ShapeDtypeStruct((orders_dev, 4, 2, degrees), F32),
        compiler_params=pltpu.CompilerParams(vmem_limit_bytes=52 * 2**20),
        cost_estimate=pl.CostEstimate(
            flops=2 * orders_dev * 256 * degrees * cycles,
            bytes_accessed=legendre.size * 2 + 2**21,
            transcendentals=0,
        ),
        name="backward",
    )(place, at_orders, *profiles, legendre)


def swapped(value, bit):
    return lax.ppermute(value, "node", [(i, i ^ bit) for i in range(lax.axis_size("node"))])


def on_device(harmonics, radial, node_weight, legendre, order_table, cycle_table):
    pixels = 4 * NSIDE
    groups = lax.axis_size("node")
    owners = lax.axis_size("sht")
    outgoing = forward(harmonics, radial, legendre)
    outgoing, radial, node_weight, order_table, cycle_table = lax.optimization_barrier(
        (outgoing, radial, node_weight, order_table, cycle_table)
    )
    arrived = lax.all_to_all(outgoing, "sht", 0, 0, tiled=True)
    parity = jnp.tile(((cycle_table - NSIDE + 1) % 2).astype(F32), 8)[None]
    turn = rotation(order_table, pixels)
    synth, analysis = tables(order_table, pixels)
    radial, analysis = lax.optimization_barrier((radial, analysis))
    profile = radial * node_weight[:, None, None] * jnp.array([2.0, 4.0], F32)[None, :, None]
    near = jnp.stack([profile] + [swapped(profile, bit) for bit in (1, 2, 3)])
    far = swapped(near, 4)
    returning = cells(arrived, synth, analysis, turn, parity)
    returning, far = lax.optimization_barrier((returning, far))
    returning = returning.reshape(owners * groups, 16, LANES)
    at_orders = lax.all_to_all(returning, ("sht", "node"), 0, 0, tiled=True)
    at_orders = at_orders.reshape(owners, groups, 16, LANES)
    node = lax.axis_index("node").astype(jnp.int32)
    place = jnp.stack([node // 4, node % 4])
    return backward(place, at_orders, (near, far), legendre)


def solution(mesh):
    in_specs = (
        P("sht", None, None, None),
        P("node", None, None),
        P("node"),
        P("sht", None, None),
        P(),
        P("sht"),
    )
    out_specs = P("sht", "node", None, None)
    return jax.shard_map(
        on_device, mesh=mesh, in_specs=in_specs, out_specs=out_specs, check_vma=False
    )
```
